32 devices in a mesh: tensor: 4 (over y, x), request: 8 (over z, core).
Axes of the slice: x: 2, y: 2, z: 4, core: 2. Of those that a mesh axis runs over, the one named last changes fastest.
Arguments:
- hidden: bfloat16 [64, 2048], P('request'), may hold values from -6 to 6
- norm_gain: float32 [2048], replicated, may hold values from 0.1 to 1.9
- w_query: bfloat16 [2048, 2048], P(None, 'tensor'), may hold values from -0.125 to 0.125
- w_keyval: bfloat16 [2048, 512], P(None, 'tensor'), may hold values from -0.125 to 0.125
- w_output: bfloat16 [2048, 2048], P('tensor'), may hold values from -0.125 to 0.125
- node_cache: bfloat16 [8, 4, 512, 128], P('request', 'tensor'), may hold values from -300 to 300
- leaf_cache: bfloat16 [64, 4, 128, 128], P('request', 'tensor'), may hold values from -300 to 300
- leaf_branch: int32 [64], replicated, may hold values from 0 to 3
- branch_root: int32 [4], replicated, may hold values from 0 to 1
- root_owner: int32 [2], replicated, may hold values from 0 to 7, as said below
- branch_owner: int32 [4], replicated, may hold values from 1 to 6, as said below
- root_len: int32 [2], replicated, may hold values from 1 to 512, as said below
- branch_len: int32 [4], replicated, may hold values from 1 to 512, as said below
- leaf_len: int32 [64], P('request'), may hold values from 0 to 127, as said below
Outputs:
- mixed: bfloat16 [64, 2048], P('request', 'tensor')
- new_entries: bfloat16 [64, 4, 128], P('request', 'tensor')
The draws below stay inside these ranges and needn't reach their ends.
Inputs may be any that keep to these rules, and one draw needn't show every extreme that they name: The 2 entries of root_owner are all different slots. `branch_owner`: different from every entry of root_owner and from one another. `root_len`: some root has exactly 512 positions. `branch_len`: some branch has exactly 512 positions. `leaf_len`: some leaf has exactly 127 positions.
All inputs are finite; a program needn't handle non-finite values.
Results may differ from the reference program's by a relative error of at most 0.029.
Values may be sent and summed in bfloat16 or wider, within the bound.
A program may use at most 128 MiB of HBM per device.

```python
import math
import jax
import jax.numpy as jnp
import numpy as np
from jax import lax

D = 2048
KV_HEADS = 4
HEAD_DIM = 64
HEADS = 32
GROUP = 8
NODE_LEN = 512
LEAF_LEN = 128
LEAVES = 64
ROOTS = 2
BRANCHES = 4
SLOTS = 8


def owner_table(key):
    key_middle = jax.random.fold_in(key, 5)
    key_roots = jax.random.fold_in(key, 6)
    key_branches = jax.random.fold_in(key, 7)
    middle = (2 + jax.random.permutation(key_middle, SLOTS - 4)).astype(jnp.int32)
    roots = jnp.concatenate([jnp.array([0, SLOTS - 1], jnp.int32), middle[:ROOTS - 2]])
    branches = jnp.concatenate([jnp.array([1, SLOTS - 2], jnp.int32), middle[ROOTS - 2:ROOTS + BRANCHES - 4]])
    roots = jnp.take(roots, jax.random.permutation(key_roots, ROOTS))
    branches = jnp.take(branches, jax.random.permutation(key_branches, BRANCHES))
    return (roots.astype(jnp.int32), branches.astype(jnp.int32))


def heavy_lengths(key, count, ceiling, lowest):
    key_level, key_value, key_place = jax.random.split(key, 3)
    level = jax.random.randint(key_level, (count,), 0, 4)
    limit = jnp.maximum(jnp.right_shift(jnp.full((count,), ceiling, jnp.int32), level), 1)
    values = lowest + jax.random.randint(key_value, (count,), 0, limit)
    spot = jax.random.randint(key_place, (), 0, count)
    return jnp.where(jnp.arange(count) == spot, lowest + ceiling - 1, values).astype(jnp.int32)


def cache_values(key, shape):
    key_base = jax.random.fold_in(key, 0)
    key_value = jax.random.fold_in(key, 2)
    lead = shape[:-1]
    half_dim = shape[-1] // 2
    key_rows = 2.0 * jnp.clip(jax.random.normal(key_base, lead + (half_dim,), jnp.float32), -6.0, 6.0)
    value_rows = jnp.clip(jax.random.normal(key_value, lead + (half_dim,), jnp.float32), -6.0, 6.0)
    return jnp.concatenate([key_rows, value_rows], -1)


def draw_root_owner(key, part):
    return owner_table(key)[0]


def draw_branch_owner(key, part):
    return owner_table(key)[1]


def draw_root_len(key, part):
    return heavy_lengths(jax.random.fold_in(key, 11), ROOTS, NODE_LEN, 1)


def draw_branch_len(key, part):
    return heavy_lengths(jax.random.fold_in(key, 12), BRANCHES, NODE_LEN, 1)


def draw_leaf_len(key, part):
    return heavy_lengths(jax.random.fold_in(key, 13), LEAVES, LEAF_LEN, 0)


def draw_node_cache(key, part):
    return cache_values(jax.random.fold_in(key, 21), (SLOTS, KV_HEADS, NODE_LEN, 2 * HEAD_DIM)).astype(jnp.bfloat16)


def draw_leaf_cache(key, part):
    return cache_values(jax.random.fold_in(key, 22), (LEAVES, KV_HEADS, LEAF_LEN, 2 * HEAD_DIM)).astype(jnp.bfloat16)


def plant(values, rng, low, top_value):
    index_at = [jax.random.randint(jax.random.fold_in(rng, axis), (), 0, length) for axis, length in enumerate(values.shape)]
    main_axis = values.shape.index(max(values.shape))
    beside = index_at[:main_axis] + [(index_at[main_axis] + 1) % values.shape[main_axis]] + index_at[main_axis + 1:]
    return values.at[tuple(index_at)].set(low).at[tuple(beside)].set(top_value)


def level_of(key, shape, cuts, smallest, top_value):
    def one(dim, blocks):
        heights = jax.random.uniform(jax.random.fold_in(jax.random.fold_in(key, 6), dim), (blocks,), jnp.float32, smallest / len(cuts), top_value / len(cuts))
        return jnp.repeat(jnp.exp(heights), shape[dim] // blocks).reshape((-1,) + (1,) * (len(shape) - dim - 1))

    loudness = one(*cuts[0])
    for cut in cuts[1:]:
        loudness = loudness * one(*cut)
    return loudness


def cumulative_ranks(amount, slope):
    portions = [(1 << 20) // math.isqrt(rank ** slope) + 1 for rank in range(1, amount + 1)]
    spread = 1 + sum(portions) // (1 << 30)
    return np.cumsum(np.array([max(1, weight // spread) for weight in portions]))


def skewed_ids(stream_key, shape, number_of, lean):
    grid = cumulative_ranks(number_of, lean)
    pick = jax.random.randint(jax.random.fold_in(stream_key, 1), shape, 0, int(grid[number_of - 1]))
    rank = jnp.searchsorted(jnp.asarray(grid, jnp.int32), pick, side="right")
    return jax.random.permutation(jax.random.fold_in(stream_key, 2), number_of)[rank].astype(jnp.int32)


def scatter_about(own_key, extent, width, bound, cuts=(), kind=jnp.bfloat16):
    drawn = width * jax.random.normal(own_key, extent, jnp.float32)
    if cuts:
        drawn = drawn * level_of(own_key, extent, cuts, -0.22, 0.18)
    return jnp.clip(drawn, -bound, bound).astype(kind)


def setup_inputs(seed: int = 0) -> dict:
    key_of = jax.random.split(jax.random.key(seed), 15)
    hidden = scatter_about(key_of[0], (LEAVES, D), 1.0, 6.0, ((0, 8),))
    norm_gain = jnp.clip(1.0 + 0.18 * jax.random.normal(key_of[1], (D,), jnp.float32), 0.1, 1.9)
    w_query = scatter_about(key_of[2], (D, HEADS * HEAD_DIM), D ** -0.5, 0.125, ((1, 4),))
    w_keyval = scatter_about(key_of[3], (D, KV_HEADS * 2 * HEAD_DIM), D ** -0.5, 0.125, ((1, 4),))
    w_output = scatter_about(key_of[4], (HEADS * HEAD_DIM, D), (HEADS * HEAD_DIM) ** -0.5, 0.125, ((0, 4),))
    node_cache = draw_node_cache(jax.random.fold_in(key_of[14], 71), 0)
    leaf_cache = draw_leaf_cache(jax.random.fold_in(key_of[14], 71), 0)
    leaf_branch = plant(skewed_ids(key_of[7], (LEAVES,), BRANCHES, 2), jax.random.fold_in(key_of[7], 3), 0, BRANCHES - 1).astype(jnp.int32)
    branch_root = plant(skewed_ids(key_of[8], (BRANCHES,), ROOTS, 1), jax.random.fold_in(key_of[8], 3), 0, ROOTS - 1).astype(jnp.int32)
    root_owner = draw_root_owner(jax.random.fold_in(key_of[14], 71), 0)
    branch_owner = draw_branch_owner(jax.random.fold_in(key_of[14], 71), 0)
    root_len = draw_root_len(jax.random.fold_in(key_of[14], 71), 0)
    branch_len = draw_branch_len(jax.random.fold_in(key_of[14], 71), 0)
    leaf_len = draw_leaf_len(jax.random.fold_in(key_of[14], 71), 0)
    return dict(hidden=hidden, norm_gain=norm_gain, w_query=w_query, w_keyval=w_keyval, w_output=w_output, node_cache=node_cache, leaf_cache=leaf_cache, leaf_branch=leaf_branch, branch_root=branch_root, root_owner=root_owner, branch_owner=branch_owner, root_len=root_len, branch_len=branch_len, leaf_len=leaf_len)


FLOOR = -1e+30

def rotate(values_in, positions):
    half_dim = values_in.shape[-1] // 2
    inverse_freq = 10000.0 ** (-(jnp.arange(half_dim, dtype=jnp.float32) * 2.0 / values_in.shape[-1]))
    angles = positions.astype(jnp.float32)[..., None] * inverse_freq
    angles = jnp.concatenate([angles, angles], -1)
    turned = jnp.concatenate([-values_in[..., half_dim:], values_in[..., :half_dim]], -1)
    return values_in * jnp.cos(angles) + turned * jnp.sin(angles)

def part_of(query_rows, cache_rows, length):
    factor = HEAD_DIM ** (-0.5)
    scores = jnp.einsum('hgd,hkd->hgk', query_rows.astype(jnp.float32), cache_rows[..., :HEAD_DIM].astype(jnp.float32)) * factor
    usable = (jnp.arange(cache_rows.shape[1], dtype=jnp.int32) < length)[None, None, :]
    scores = jnp.where(usable, scores, FLOOR)
    peak = lax.optimization_barrier(jnp.max(scores, -1))
    weights = jnp.where(usable, jnp.exp(scores - peak[..., None]), 0.0).astype(jnp.bfloat16)
    summed = jnp.einsum('hgk,hkd->hgd', weights.astype(jnp.float32), cache_rows[..., HEAD_DIM:].astype(jnp.float32))
    weight_sum = lax.optimization_barrier(jnp.sum(weights.astype(jnp.float32), -1))
    return (summed, weight_sum, peak)

def reference(hidden, norm_gain, w_query, w_keyval, w_output, node_cache, leaf_cache, leaf_branch, branch_root, root_owner, branch_owner, root_len, branch_len, leaf_len):
    widened = hidden.astype(jnp.float32)
    normed = (widened * lax.rsqrt(lax.optimization_barrier(jnp.mean(widened * widened, -1, keepdims=True)) + 1e-05) * norm_gain).astype(jnp.bfloat16)
    leaf_root = branch_root[leaf_branch]
    positions = root_len[leaf_root] + branch_len[leaf_branch] + leaf_len
    raw_query = jnp.dot(normed, w_query, preferred_element_type=jnp.float32).reshape(LEAVES, KV_HEADS, GROUP, HEAD_DIM)
    queries = rotate(raw_query, positions[:, None, None]).astype(jnp.bfloat16)
    raw_entry = jnp.dot(normed, w_keyval, preferred_element_type=jnp.float32).reshape(LEAVES, KV_HEADS, 2 * HEAD_DIM)
    new_entries = jnp.concatenate([rotate(raw_entry[..., :HEAD_DIM], positions[:, None]), raw_entry[..., HEAD_DIM:]], -1).astype(jnp.bfloat16)

    def one_leaf(leaf_index):
        branch = leaf_branch[leaf_index]
        root_id = branch_root[branch]
        own_query = queries[leaf_index]
        length = leaf_len[leaf_index]
        marker = (jnp.arange(leaf_cache.shape[2], dtype=jnp.int32) == length)[None, :, None]
        appended = jnp.where(marker, new_entries[leaf_index][:, None, :], leaf_cache[leaf_index])
        pieces = [part_of(own_query, node_cache[root_owner[root_id]], root_len[root_id]), part_of(own_query, node_cache[branch_owner[branch]], branch_len[branch]), part_of(own_query, appended, length + 1)]
        peak = jnp.maximum(jnp.maximum(pieces[0][2], pieces[1][2]), pieces[2][2])
        numerator = jnp.zeros(peak.shape + (HEAD_DIM,), jnp.float32)
        denominator = jnp.zeros(peak.shape, jnp.float32)
        for summed, weight_sum, part_peak in pieces:
            scaled = jnp.exp(part_peak - peak)
            numerator = numerator + scaled[..., None] * summed
            denominator = denominator + scaled * weight_sum
        return (numerator / denominator[..., None]).astype(jnp.bfloat16)
    attended = lax.map(one_leaf, jnp.arange(LEAVES, dtype=jnp.int32)).reshape(LEAVES, HEADS * HEAD_DIM)
    mixed = jnp.dot(attended, w_output, preferred_element_type=jnp.float32).astype(jnp.bfloat16)
    return (mixed, new_entries)
```

```python
import functools

import jax
import jax.numpy as jnp
import numpy as np
from jax import lax
from jax.experimental import pallas as pl
from jax.experimental.pallas import tpu as pltpu
from jax.sharding import PartitionSpec as P

FLOOR = -1e30
MESH = pl.DeviceIdType.MESH
F32 = jnp.float32
BF16 = jnp.bfloat16
LANES = 128
NT = (((1,), (1,)), ((), ()))
NN = (((1,), (0,)), ((), ()))


def each(low, high, step):
    if high - low <= 8:
        for k in range(low, high):
            step(k)
    else:
        lax.fori_loop(low, high, lambda k, carry: (step(k), carry)[1], 0)


def dot(a, b, dims):
    return lax.dot_general(a, b, dims, preferred_element_type=F32)


def kernel(
    n,
    nt,
    hidden,
    gain,
    freq,
    leaf_branch,
    branch_root,
    root_owner,
    branch_owner,
    root_len,
    branch_len,
    leaf_len,
    w_query,
    w_keyval,
    w_output,
    node_hbm,
    leaf_hbm,
    mixed,
    entry,
    wq,
    wkv,
    wo,
    node,
    leaf,
    q_all,
    part_out,
    part_in,
    term_out,
    term_in,
    load_sem,
    q_send,
    q_recv,
    p_send,
    p_recv,
    t_send,
    t_recv,
):
    me = lax.axis_index("request")
    mine = lax.axis_index("tensor")
    rows, width = hidden.shape
    head_dim = LANES // 2
    chunks = wq.shape[1] // LANES
    body_rows = chunks * rows
    factor = head_dim ** (-0.5)
    splits = 4
    depth = width // splits
    cols = wo.shape[2]

    loads = []

    def load(src, dst):
        copy = pltpu.make_async_copy(src, dst, load_sem.at[len(loads)])
        copy.start()
        loads.append(copy)
        return copy

    q_loads = []
    for s in range(splits):
        part = pl.ds(s * depth, depth)
        q_loads.append(
            (load(w_query.at[part], wq.at[part]), load(w_keyval.at[part], wkv.at[part]))
        )
    node_load = load(node_hbm, node)
    leaf_load = load(leaf_hbm, leaf)
    o_loads = []
    for k in range(nt):
        target = lax.rem(mine + k, nt)
        o_loads.append(
            load(w_output.at[:, pl.ds(pl.multiple_of(target * cols, cols), cols)], wo.at[k])
        )

    barrier = pltpu.get_barrier_semaphore()

    def greet(k):
        pl.semaphore_signal(
            barrier, inc=1, device_id=(mine, lax.rem(me + k, n)), device_id_type=MESH
        )

    each(1, n, greet)
    for k in range(1, nt):
        pl.semaphore_signal(
            barrier, inc=1, device_id=(lax.rem(mine + k, nt), me), device_id_type=MESH
        )

    row8 = lax.broadcasted_iota(jnp.int32, (rows, LANES), 0)
    lane8 = lax.broadcasted_iota(jnp.int32, (rows, LANES), 1)
    low8 = lane8 < head_dim
    position = jnp.zeros((rows, LANES), jnp.int32)
    lengths = jnp.zeros((rows, LANES), jnp.int32)
    root_slot, branch_slot = [], []
    for l in range(rows):
        b = leaf_branch[me * rows + l]
        r = branch_root[b]
        own = leaf_len[l]
        position = jnp.where(row8 == l, root_len[r] + branch_len[b] + own, position)
        lengths = jnp.where(row8 == l, own, lengths)
        root_slot.append(lax.rem(root_owner[r] - me + n, n))
        branch_slot.append(lax.rem(branch_owner[b] - me + n, n))
    my_length = jnp.int32(0)
    for owner, length in ((root_owner, root_len), (branch_owner, branch_len)):
        for j in range(owner.shape[0]):
            my_length = my_length + jnp.where(owner[j] == me, length[j], 0)
    angles = position.astype(F32) * freq[...]
    cosine, sine = jnp.cos(angles), jnp.sin(angles)
    first_half = lax.rem(lane8, head_dim) < head_dim // 2

    def rotate(x):
        up = pltpu.roll(x, LANES - head_dim // 2, 1)
        down = pltpu.roll(x, head_dim // 2, 1)
        return x * cosine + jnp.where(first_half, -up, down) * sine

    widened = hidden[...].astype(F32)
    mean = jnp.sum(widened * widened, -1, keepdims=True) * (1.0 / width)
    normed = (widened * lax.rsqrt(mean + 1e-05) * gain[...]).astype(BF16)
    raw = jnp.zeros((rows, wq.shape[1]), F32)
    raw_entry = jnp.zeros((rows, LANES), F32)
    for s in range(splits):
        for copy in q_loads[s]:
            copy.wait()
        part = slice(s * depth, (s + 1) * depth)
        raw = raw + dot(normed[:, part], wq[part, :], NN)
        raw_entry = raw_entry + dot(normed[:, part], wkv[part, :], NN)
    queries = jnp.concatenate(
        [rotate(raw[:, c * LANES : (c + 1) * LANES]) * factor for c in range(chunks)], 0
    ).astype(BF16)
    q_all[0] = queries

    pl.semaphore_wait(barrier, n - 1 + nt - 1)

    def q_copy(k):
        return pltpu.make_async_remote_copy(
            src_ref=q_all.at[0],
            dst_ref=q_all.at[k],
            send_sem=q_send.at[k],
            recv_sem=q_recv.at[k],
            device_id=(mine, lax.rem(me + k, n)),
            device_id_type=MESH,
        )

    each(1, n, lambda k: q_copy(k).start())

    entry_new = jnp.where(low8, rotate(raw_entry), raw_entry).astype(BF16)
    entry[...] = entry_new
    new32 = entry_new.astype(F32)
    swapped = pltpu.roll(new32, head_dim, 1)
    new_key = jnp.where(low8, new32, swapped)
    new_value = jnp.where(low8, swapped, new32)

    def split_rows(rows_in):
        wide = rows_in.astype(F32)
        turned = pltpu.roll(wide, head_dim, 1)
        low = lax.broadcasted_iota(jnp.int32, wide.shape, 1) < head_dim
        keys = (jnp.where(low, wide, 0.0).astype(BF16), jnp.where(low, 0.0, turned).astype(BF16))
        values = (jnp.where(low, turned, 0.0).astype(BF16), jnp.where(low, 0.0, wide).astype(BF16))
        return keys, values

    node_load.wait()
    node_keys, node_values = split_rows(node[...])

    leaf_load.wait()
    leaf_keys, leaf_values = split_rows(leaf[...])
    per_leaf = leaf.shape[0] // rows
    column = lax.broadcasted_iota(jnp.int32, (rows, leaf.shape[0]), 1)
    start = lax.broadcasted_iota(jnp.int32, (rows, leaf.shape[0]), 0) * per_leaf
    usable = (column >= start) & (column < start + lengths[:, :1])
    q32 = queries.astype(F32)
    leaf_stats = [jnp.zeros((rows, LANES), F32), jnp.zeros((rows, LANES), F32)]
    leaf_sum = []
    leaf_scores = [dot(queries, keys, NT) for keys in leaf_keys]
    leaf_weights = [[], []]
    fresh = []
    for c in range(chunks):
        part = slice(c * rows, (c + 1) * rows)
        product = q32[part] * new_key
        pair = []
        for e in range(2):
            score = jnp.sum(jnp.where(low8 if e == 0 else ~low8, product, 0.0), -1, keepdims=True)
            scores = jnp.where(usable, leaf_scores[e][part], FLOOR)
            peak = jnp.maximum(jnp.max(scores, -1, keepdims=True), score)
            weights = jnp.exp(scores - peak).astype(BF16).astype(F32)
            weight = jnp.exp(score - peak).astype(BF16).astype(F32)
            total = jnp.sum(weights, -1, keepdims=True) + weight
            leaf_weights[e].append(weights)
            pair.append(weight)
            here = lane8 == 2 * c + e
            leaf_stats[0] = jnp.where(here, peak, leaf_stats[0])
            leaf_stats[1] = jnp.where(here, total, leaf_stats[1])
        fresh.append(jnp.where(low8, pair[0], pair[1]) * new_value)
    leaf_sum = jnp.concatenate(fresh, 0)
    for e in range(2):
        leaf_sum = leaf_sum + dot(
            jnp.concatenate(leaf_weights[e], 0).astype(BF16), leaf_values[e], NN
        )

    block = min(n, 8)

    def p_copy(k):
        return pltpu.make_async_remote_copy(
            src_ref=part_out.at[k],
            dst_ref=part_in.at[k],
            send_sem=p_send.at[k],
            recv_sem=p_recv.at[k],
            device_id=(mine, lax.rem(me - k + n, n)),
            device_id_type=MESH,
        )

    held = lax.broadcasted_iota(jnp.int32, (block * body_rows, node.shape[0]), 1) < my_length

    def owner_block(first):
        rows_query = q_all[pl.ds(first, block)].reshape(block * body_rows, LANES)
        summed = None
        peaks, totals = [], []
        for e in range(2):
            scores = jnp.where(held, dot(rows_query, node_keys[e], NT), FLOOR)
            peak = jnp.max(scores, -1, keepdims=True)
            weights = jnp.exp(scores - peak).astype(BF16)
            peaks.append(peak)
            totals.append(jnp.sum(weights.astype(F32), -1, keepdims=True))
            term = dot(weights, node_values[e], NN)
            summed = term if summed is None else summed + term
        for j in range(block):
            stats = jnp.zeros((rows, LANES), F32)
            for c in range(chunks):
                at = j * body_rows + c * rows
                for e in range(2):
                    lane = 2 * c + e
                    stats = jnp.where(lane8 == lane, peaks[e][at : at + rows], stats)
                    stats = jnp.where(lane8 == 2 * chunks + lane, totals[e][at : at + rows], stats)
            high = stats.astype(BF16).astype(F32)
            middle = (stats - high).astype(BF16).astype(F32)
            small = (stats - high) - middle
            part_out[first + j] = jnp.concatenate(
                [
                    summed[j * body_rows : (j + 1) * body_rows],
                    jnp.where(low8, high, pltpu.roll(small, head_dim, 1)),
                    middle,
                ],
                0,
            ).astype(BF16)

    each(1, n, lambda k: q_copy(k).wait_recv())
    for first in range(0, n, block):
        if n == block:
            owner_block(0)
        elif first == 0:
            lax.fori_loop(
                0,
                n // block,
                lambda i, carry: (owner_block(i * block), carry)[1],
                0,
            )
    each(1, n, lambda k: p_copy(k).start())
    part_in[0] = part_out[0]
    each(1, n, lambda k: p_copy(k).wait_recv())

    row_of = lax.rem(lax.broadcasted_iota(jnp.int32, part_in.shape[1:], 0), rows)

    def pick(slots):
        chosen = part_in[slots[0]].astype(F32)
        for l in range(1, rows):
            chosen = jnp.where(row_of == l, part_in[slots[l]].astype(F32), chosen)
        high = chosen[body_rows : body_rows + rows]
        stats = (high + chosen[body_rows + rows :]) + pltpu.roll(high, head_dim, 1)
        return chosen[:body_rows], stats, pltpu.roll(stats, LANES - 2 * chunks, 1)

    parts = [pick(root_slot), pick(branch_slot), (leaf_sum, leaf_stats[0], leaf_stats[1])]
    top = jnp.maximum(jnp.maximum(parts[0][1], parts[1][1]), parts[2][1])
    scales = [jnp.exp(p[1] - top) for p in parts]
    bottom = scales[0] * parts[0][2] + scales[1] * parts[1][2] + scales[2] * parts[2][2]
    scales = [s / bottom for s in scales]
    attended = []
    for c in range(chunks):
        part = slice(c * rows, (c + 1) * rows)
        total = None
        for p, s in zip(parts, scales):
            spread = jnp.where(low8, s[:, 2 * c : 2 * c + 1], s[:, 2 * c + 1 : 2 * c + 2])
            term = spread * p[0][part]
            total = term if total is None else total + term
        attended.append(total)
    attended = jnp.concatenate(attended, 1).astype(BF16)

    def t_copy(k):
        return pltpu.make_async_remote_copy(
            src_ref=term_out.at[k],
            dst_ref=term_in.at[k],
            send_sem=t_send.at[k],
            recv_sem=t_recv.at[k],
            device_id=(lax.rem(mine + k, nt), me),
            device_id_type=MESH,
        )

    out_chunks = cols // LANES
    own_term = None
    for k in [*range(1, nt), 0]:
        o_loads[k].wait()
        term = dot(attended, wo[k], NN)
        if k == 0:
            own_term = term
        else:
            term_out[k] = jnp.concatenate(
                [term[:, c * LANES : (c + 1) * LANES] for c in range(out_chunks)], 0
            ).astype(BF16)
            t_copy(k).start()
    for k in range(1, nt):
        t_copy(k).wait_recv()
    for c in range(out_chunks):
        part = slice(c * LANES, (c + 1) * LANES)
        total = own_term[:, part]
        for k in range(1, nt):
            total = total + term_in[k].astype(F32)[c * rows : (c + 1) * rows]
        mixed[:, part] = total.astype(BF16)

    each(1, n, lambda k: q_copy(k).wait_send())
    each(1, n, lambda k: p_copy(k).wait_send())
    for k in range(1, nt):
        t_copy(k).wait_send()


def local(
    n,
    nt,
    hidden,
    norm_gain,
    w_query,
    w_keyval,
    w_output,
    node_cache,
    leaf_cache,
    leaf_branch,
    branch_root,
    root_owner,
    branch_owner,
    root_len,
    branch_len,
    leaf_len,
):
    rows, width = hidden.shape
    head_dim = w_keyval.shape[1] // 2
    inner = w_query.shape[1]
    cols = w_output.shape[1] // nt
    power = (np.arange(LANES) % (head_dim // 2)) * 2.0 / head_dim
    freq = jnp.asarray((10000.0 ** (-power)).astype(np.float32)[None, :])
    node = node_cache.reshape(-1, LANES)
    leaf = leaf_cache.reshape(-1, LANES)
    body_rows = inner // LANES * rows
    vmem = pl.BlockSpec(memory_space=pltpu.VMEM)
    smem = pl.BlockSpec(memory_space=pltpu.SMEM)
    anywhere = pl.BlockSpec(memory_space=pl.ANY)
    dma = pltpu.SemaphoreType.DMA
    mixed, entry = pl.pallas_call(
        functools.partial(kernel, n, nt),
        out_shape=(
            jax.ShapeDtypeStruct((rows, cols), BF16),
            jax.ShapeDtypeStruct((rows, LANES), BF16),
        ),
        in_specs=[vmem] * 3 + [smem] * 7 + [anywhere] * 5,
        out_specs=(vmem, vmem),
        scratch_shapes=[
            pltpu.VMEM(w_query.shape, BF16),
            pltpu.VMEM(w_keyval.shape, BF16),
            pltpu.VMEM((nt, inner, cols), BF16),
            pltpu.VMEM(node.shape, BF16),
            pltpu.VMEM(leaf.shape, BF16),
            pltpu.VMEM((n, body_rows, LANES), BF16),
            pltpu.VMEM((n, body_rows + 2 * rows, LANES), BF16),
            pltpu.VMEM((n, body_rows + 2 * rows, LANES), BF16),
            pltpu.VMEM((nt, cols // LANES * rows, LANES), BF16),
            pltpu.VMEM((nt, cols // LANES * rows, LANES), BF16),
            dma((8 + 2 + nt,)),
            dma((n,)),
            dma((n,)),
            dma((n,)),
            dma((n,)),
            dma((nt,)),
            dma((nt,)),
        ],
        compiler_params=pltpu.CompilerParams(
            collective_id=0, has_side_effects=True, vmem_limit_bytes=40 * 1024 * 1024
        ),
    )(
        hidden,
        norm_gain[None, :],
        freq,
        leaf_branch,
        branch_root,
        root_owner,
        branch_owner,
        root_len,
        branch_len,
        leaf_len,
        w_query,
        w_keyval,
        w_output,
        node,
        leaf,
    )
    return (mixed, entry[:, None, :])


def solution(mesh):
    in_specs = (
        P("request", None),
        P(),
        P(None, "tensor"),
        P(None, "tensor"),
        P("tensor", None),
        P("request", "tensor", None, None),
        P("request", "tensor", None, None),
        P(),
        P(),
        P(),
        P(),
        P(),
        P(),
        P("request"),
    )
    out_specs = (P("request", "tensor"), P("request", "tensor", None))
    run = functools.partial(local, mesh.shape["request"], mesh.shape["tensor"])
    return jax.shard_map(run, mesh=mesh, in_specs=in_specs, out_specs=out_specs, check_vma=False)
```

```python
import functools

import jax
import jax.numpy as jnp
import numpy as np
from jax import lax
from jax.experimental import pallas as pl
from jax.experimental.pallas import tpu as pltpu
from jax.sharding import PartitionSpec as P

FLOOR = -1e30
MESH = pl.DeviceIdType.MESH
F32 = jnp.float32
BF16 = jnp.bfloat16
LANES = 128
NT = (((1,), (1,)), ((), ()))
NN = (((1,), (0,)), ((), ()))


def each(low, high, step):
    if high - low <= 8:
        for k in range(low, high):
            step(k)
    else:
        lax.fori_loop(low, high, lambda k, carry: (step(k), carry)[1], 0)


def dot(a, b, dims):
    return lax.dot_general(a, b, dims, preferred_element_type=F32)


def kernel(
    n,
    nt,
    hidden_hbm,
    gain_hbm,
    freq_hbm,
    leaf_branch_hbm,
    branch_root_hbm,
    root_owner_hbm,
    branch_owner_hbm,
    root_len_hbm,
    branch_len_hbm,
    leaf_len_hbm,
    w_query,
    w_keyval,
    w_output,
    node_hbm,
    leaf_hbm,
    result,
    hidden,
    gain,
    freq,
    leaf_branch,
    branch_root,
    root_owner,
    branch_owner,
    root_len,
    branch_len,
    leaf_len,
    wq,
    wkv,
    wo,
    node,
    leaf,
    q_all,
    part_out,
    part_in,
    term_out,
    term_in,
    load_sem,
    q_send,
    q_recv,
    p_send,
    p_recv,
    t_send,
    t_recv,
):
    me = lax.axis_index("request")
    mine = lax.axis_index("tensor")
    rows, width = hidden.shape
    head_dim = LANES // 2
    chunks = wq.shape[1] // LANES
    body_rows = chunks * rows
    factor = head_dim ** (-0.5)
    splits = 4
    depth = width // splits
    cols = wo.shape[2]

    loads = []

    def load(src, dst):
        copy = pltpu.make_async_copy(src, dst, load_sem.at[len(loads)])
        copy.start()
        loads.append(copy)
        return copy

    index_loads = [
        load(leaf_branch_hbm, leaf_branch),
        load(branch_root_hbm, branch_root),
        load(root_len_hbm, root_len),
        load(branch_len_hbm, branch_len),
        load(leaf_len_hbm, leaf_len),
        load(root_owner_hbm, root_owner),
        load(branch_owner_hbm, branch_owner),
        load(freq_hbm, freq),
    ]
    row_loads = [load(hidden_hbm, hidden), load(gain_hbm, gain)]
    q_loads = []
    for s in range(splits):
        part = pl.ds(s * depth, depth)
        q_loads.append(
            (load(w_query.at[part], wq.at[part]), load(w_keyval.at[part], wkv.at[part]))
        )
    node_load = load(node_hbm, node)
    leaf_load = load(leaf_hbm, leaf)
    o_loads = []
    for k in range(nt):
        target = lax.rem(mine + k, nt)
        o_loads.append(
            load(w_output.at[:, pl.ds(pl.multiple_of(target * cols, cols), cols)], wo.at[k])
        )

    barrier = pltpu.get_barrier_semaphore()

    def greet(k):
        pl.semaphore_signal(
            barrier, inc=1, device_id=(mine, lax.rem(me + k, n)), device_id_type=MESH
        )

    each(1, n, greet)
    for k in range(1, nt):
        pl.semaphore_signal(
            barrier, inc=1, device_id=(lax.rem(mine + k, nt), me), device_id_type=MESH
        )

    for copy in index_loads:
        copy.wait()
    row8 = lax.broadcasted_iota(jnp.int32, (rows, LANES), 0)
    lane8 = lax.broadcasted_iota(jnp.int32, (rows, LANES), 1)
    low8 = lane8 < head_dim
    position = jnp.zeros((rows, LANES), jnp.int32)
    lengths = jnp.zeros((rows, LANES), jnp.int32)
    root_slot, branch_slot = [], []
    for l in range(rows):
        b = leaf_branch[me * rows + l]
        r = branch_root[b]
        own = leaf_len[l]
        position = jnp.where(row8 == l, root_len[r] + branch_len[b] + own, position)
        lengths = jnp.where(row8 == l, own, lengths)
        root_slot.append(lax.rem(root_owner[r] - me + n, n))
        branch_slot.append(lax.rem(branch_owner[b] - me + n, n))
    my_length = jnp.int32(0)
    for owner, length in ((root_owner, root_len), (branch_owner, branch_len)):
        for j in range(owner.shape[0]):
            my_length = my_length + jnp.where(owner[j] == me, length[j], 0)
    angles = position.astype(F32) * freq[...]
    cosine, sine = jnp.cos(angles), jnp.sin(angles)
    first_half = lax.rem(lane8, head_dim) < head_dim // 2

    def rotate(x):
        up = pltpu.roll(x, LANES - head_dim // 2, 1)
        down = pltpu.roll(x, head_dim // 2, 1)
        return x * cosine + jnp.where(first_half, -up, down) * sine

    for copy in row_loads:
        copy.wait()
    widened = hidden[...].astype(F32)
    mean = jnp.sum(widened * widened, -1, keepdims=True) * (1.0 / width)
    normed = (widened * lax.rsqrt(mean + 1e-05) * gain[...]).astype(BF16)
    raw = jnp.zeros((rows, wq.shape[1]), F32)
    raw_entry = jnp.zeros((rows, LANES), F32)
    for s in range(splits):
        for copy in q_loads[s]:
            copy.wait()
        part = slice(s * depth, (s + 1) * depth)
        raw = raw + dot(normed[:, part], wq[part, :], NN)
        raw_entry = raw_entry + dot(normed[:, part], wkv[part, :], NN)
    queries = jnp.concatenate(
        [rotate(raw[:, c * LANES : (c + 1) * LANES]) * factor for c in range(chunks)], 0
    ).astype(BF16)
    q_all[0] = queries

    pl.semaphore_wait(barrier, n - 1 + nt - 1)

    def q_copy(k):
        return pltpu.make_async_remote_copy(
            src_ref=q_all.at[0],
            dst_ref=q_all.at[k],
            send_sem=q_send.at[k],
            recv_sem=q_recv.at[k],
            device_id=(mine, lax.rem(me + k, n)),
            device_id_type=MESH,
        )

    each(1, n, lambda k: q_copy(k).start())

    entry_new = jnp.where(low8, rotate(raw_entry), raw_entry).astype(BF16)
    result[:, cols:] = entry_new
    new32 = entry_new.astype(F32)
    swapped = pltpu.roll(new32, head_dim, 1)
    new_key = jnp.where(low8, new32, swapped)
    new_value = jnp.where(low8, swapped, new32)

    def split_rows(rows_in):
        wide = rows_in.astype(F32)
        turned = pltpu.roll(wide, head_dim, 1)
        low = lax.broadcasted_iota(jnp.int32, wide.shape, 1) < head_dim
        keys = (jnp.where(low, wide, 0.0).astype(BF16), jnp.where(low, 0.0, turned).astype(BF16))
        values = (jnp.where(low, turned, 0.0).astype(BF16), jnp.where(low, 0.0, wide).astype(BF16))
        return keys, values

    node_load.wait()
    node_keys, node_values = split_rows(node[...])

    leaf_load.wait()
    leaf_keys, leaf_values = split_rows(leaf[...])
    per_leaf = leaf.shape[0] // rows
    column = lax.broadcasted_iota(jnp.int32, (rows, leaf.shape[0]), 1)
    start = lax.broadcasted_iota(jnp.int32, (rows, leaf.shape[0]), 0) * per_leaf
    usable = (column >= start) & (column < start + lengths[:, :1])
    q32 = queries.astype(F32)
    leaf_stats = [jnp.zeros((rows, LANES), F32), jnp.zeros((rows, LANES), F32)]
    leaf_sum = []
    leaf_scores = [dot(queries, keys, NT) for keys in leaf_keys]
    leaf_weights = [[], []]
    fresh = []
    for c in range(chunks):
        part = slice(c * rows, (c + 1) * rows)
        product = q32[part] * new_key
        pair = []
        for e in range(2):
            score = jnp.sum(jnp.where(low8 if e == 0 else ~low8, product, 0.0), -1, keepdims=True)
            scores = jnp.where(usable, leaf_scores[e][part], FLOOR)
            peak = jnp.maximum(jnp.max(scores, -1, keepdims=True), score)
            weights = jnp.exp(scores - peak).astype(BF16).astype(F32)
            weight = jnp.exp(score - peak).astype(BF16).astype(F32)
            total = jnp.sum(weights, -1, keepdims=True) + weight
            leaf_weights[e].append(weights)
            pair.append(weight)
            here = lane8 == 2 * c + e
            leaf_stats[0] = jnp.where(here, peak, leaf_stats[0])
            leaf_stats[1] = jnp.where(here, total, leaf_stats[1])
        fresh.append(jnp.where(low8, pair[0], pair[1]) * new_value)
    leaf_sum = jnp.concatenate(fresh, 0)
    for e in range(2):
        leaf_sum = leaf_sum + dot(
            jnp.concatenate(leaf_weights[e], 0).astype(BF16), leaf_values[e], NN
        )

    block = min(n, 8)

    def p_copy(k):
        return pltpu.make_async_remote_copy(
            src_ref=part_out.at[k],
            dst_ref=part_in.at[k],
            send_sem=p_send.at[k],
            recv_sem=p_recv.at[k],
            device_id=(mine, lax.rem(me - k + n, n)),
            device_id_type=MESH,
        )

    held = lax.broadcasted_iota(jnp.int32, (block * body_rows, node.shape[0]), 1) < my_length

    def owner_block(first):
        rows_query = q_all[pl.ds(first, block)].reshape(block * body_rows, LANES)
        summed = None
        peaks, totals = [], []
        for e in range(2):
            scores = jnp.where(held, dot(rows_query, node_keys[e], NT), FLOOR)
            peak = jnp.max(scores, -1, keepdims=True)
            weights = jnp.exp(scores - peak).astype(BF16)
            peaks.append(peak)
            totals.append(jnp.sum(weights.astype(F32), -1, keepdims=True))
            term = dot(weights, node_values[e], NN)
            summed = term if summed is None else summed + term
        for j in range(block):
            stats = jnp.zeros((rows, LANES), F32)
            for c in range(chunks):
                at = j * body_rows + c * rows
                for e in range(2):
                    lane = 2 * c + e
                    stats = jnp.where(lane8 == lane, peaks[e][at : at + rows], stats)
                    stats = jnp.where(lane8 == 2 * chunks + lane, totals[e][at : at + rows], stats)
            high = stats.astype(BF16).astype(F32)
            middle = (stats - high).astype(BF16).astype(F32)
            small = (stats - high) - middle
            part_out[first + j] = jnp.concatenate(
                [
                    summed[j * body_rows : (j + 1) * body_rows],
                    jnp.where(low8, high, pltpu.roll(small, head_dim, 1)),
                    middle,
                ],
                0,
            ).astype(BF16)

    each(1, n, lambda k: q_copy(k).wait_recv())
    for first in range(0, n, block):
        if n == block:
            owner_block(0)
        elif first == 0:
            lax.fori_loop(
                0,
                n // block,
                lambda i, carry: (owner_block(i * block), carry)[1],
                0,
            )
    each(1, n, lambda k: p_copy(k).start())
    part_in[0] = part_out[0]
    each(1, n, lambda k: p_copy(k).wait_recv())

    row_of = lax.rem(lax.broadcasted_iota(jnp.int32, part_in.shape[1:], 0), rows)

    def pick(slots):
        chosen = part_in[slots[0]].astype(F32)
        for l in range(1, rows):
            chosen = jnp.where(row_of == l, part_in[slots[l]].astype(F32), chosen)
        high = chosen[body_rows : body_rows + rows]
        stats = (high + chosen[body_rows + rows :]) + pltpu.roll(high, head_dim, 1)
        return chosen[:body_rows], stats, pltpu.roll(stats, LANES - 2 * chunks, 1)

    parts = [pick(root_slot), pick(branch_slot), (leaf_sum, leaf_stats[0], leaf_stats[1])]
    top = jnp.maximum(jnp.maximum(parts[0][1], parts[1][1]), parts[2][1])
    scales = [jnp.exp(p[1] - top) for p in parts]
    bottom = scales[0] * parts[0][2] + scales[1] * parts[1][2] + scales[2] * parts[2][2]
    scales = [s / bottom for s in scales]
    attended = []
    for c in range(chunks):
        part = slice(c * rows, (c + 1) * rows)
        total = None
        for p, s in zip(parts, scales):
            spread = jnp.where(low8, s[:, 2 * c : 2 * c + 1], s[:, 2 * c + 1 : 2 * c + 2])
            term = spread * p[0][part]
            total = term if total is None else total + term
        attended.append(total)
    attended = jnp.concatenate(attended, 1).astype(BF16)

    def t_copy(k):
        return pltpu.make_async_remote_copy(
            src_ref=term_out.at[k],
            dst_ref=term_in.at[k],
            send_sem=t_send.at[k],
            recv_sem=t_recv.at[k],
            device_id=(lax.rem(mine + k, nt), me),
            device_id_type=MESH,
        )

    out_chunks = cols // LANES
    own_term = None
    for k in [*range(1, nt), 0]:
        o_loads[k].wait()
        term = dot(attended, wo[k], NN)
        if k == 0:
            own_term = term
        else:
            term_out[k] = jnp.concatenate(
                [term[:, c * LANES : (c + 1) * LANES] for c in range(out_chunks)], 0
            ).astype(BF16)
            t_copy(k).start()
    for k in range(1, nt):
        t_copy(k).wait_recv()
    for c in range(out_chunks):
        part = slice(c * LANES, (c + 1) * LANES)
        total = own_term[:, part]
        for k in range(1, nt):
            total = total + term_in[k].astype(F32)[c * rows : (c + 1) * rows]
        result[:, part] = total.astype(BF16)

    each(1, n, lambda k: q_copy(k).wait_send())
    each(1, n, lambda k: p_copy(k).wait_send())
    for k in range(1, nt):
        t_copy(k).wait_send()


def local(
    n,
    nt,
    hidden,
    norm_gain,
    w_query,
    w_keyval,
    w_output,
    node_cache,
    leaf_cache,
    leaf_branch,
    branch_root,
    root_owner,
    branch_owner,
    root_len,
    branch_len,
    leaf_len,
):
    rows, width = hidden.shape
    head_dim = w_keyval.shape[1] // 2
    inner = w_query.shape[1]
    cols = w_output.shape[1] // nt
    power = (np.arange(LANES) % (head_dim // 2)) * 2.0 / head_dim
    freq = jnp.asarray((10000.0 ** (-power)).astype(np.float32)[None, :])
    node = node_cache.reshape(-1, LANES)
    leaf = leaf_cache.reshape(-1, LANES)
    body_rows = inner // LANES * rows
    dma = pltpu.SemaphoreType.DMA
    operands = (
        hidden,
        norm_gain[None, :],
        freq,
        leaf_branch,
        branch_root,
        root_owner,
        branch_owner,
        root_len,
        branch_len,
        leaf_len,
        w_query,
        w_keyval,
        w_output,
        node,
        leaf,
    )
    result = pl.pallas_call(
        functools.partial(kernel, n, nt),
        out_shape=jax.ShapeDtypeStruct((rows, cols + LANES), BF16),
        in_specs=[pl.BlockSpec(memory_space=pltpu.HBM)] * len(operands),
        out_specs=pl.BlockSpec(memory_space=pltpu.VMEM),
        scratch_shapes=[
            *[pltpu.VMEM(a.shape, a.dtype) for a in operands[:3]],
            *[pltpu.SMEM(a.shape, a.dtype) for a in operands[3:10]],
            pltpu.VMEM(w_query.shape, BF16),
            pltpu.VMEM(w_keyval.shape, BF16),
            pltpu.VMEM((nt, inner, cols), BF16),
            pltpu.VMEM(node.shape, BF16),
            pltpu.VMEM(leaf.shape, BF16),
            pltpu.VMEM((n, body_rows, LANES), BF16),
            pltpu.VMEM((n, body_rows + 2 * rows, LANES), BF16),
            pltpu.VMEM((n, body_rows + 2 * rows, LANES), BF16),
            pltpu.VMEM((nt, cols // LANES * rows, LANES), BF16),
            pltpu.VMEM((nt, cols // LANES * rows, LANES), BF16),
            dma((10 + 8 + 2 + nt,)),
            dma((n,)),
            dma((n,)),
            dma((n,)),
            dma((n,)),
            dma((nt,)),
            dma((nt,)),
        ],
        compiler_params=pltpu.CompilerParams(
            collective_id=0, has_side_effects=True, vmem_limit_bytes=63 * 1024 * 1024
        ),
    )(*operands)
    return (result[:, :cols], result[:, None, cols:])


def solution(mesh):
    in_specs = (
        P("request", None),
        P(),
        P(None, "tensor"),
        P(None, "tensor"),
        P("tensor", None),
        P("request", "tensor", None, None),
        P("request", "tensor", None, None),
        P(),
        P(),
        P(),
        P(),
        P(),
        P(),
        P("request"),
    )
    out_specs = (P("request", "tensor"), P("request", "tensor", None))
    run = functools.partial(local, mesh.shape["request"], mesh.shape["tensor"])
    return jax.shard_map(run, mesh=mesh, in_specs=in_specs, out_specs=out_specs, check_vma=False)
```

```python
import functools

import jax
import jax.numpy as jnp
import numpy as np
from jax import lax
from jax.experimental import pallas as pl
from jax.experimental.pallas import tpu as pltpu
from jax.sharding import PartitionSpec as P

FLOOR = -1e30
MESH = pl.DeviceIdType.MESH
F32 = jnp.float32
BF16 = jnp.bfloat16
LANES = 128
NT = (((1,), (1,)), ((), ()))
NN = (((1,), (0,)), ((), ()))


def each(low, high, step):
    if high - low <= 8:
        for k in range(low, high):
            step(k)
    else:
        lax.fori_loop(low, high, lambda k, carry: (step(k), carry)[1], 0)


def dot(a, b, dims):
    return lax.dot_general(a, b, dims, preferred_element_type=F32)


def kernel(
    n,
    nt,
    hidden_hbm,
    gain_hbm,
    freq_hbm,
    leaf_branch_hbm,
    branch_root_hbm,
    root_owner_hbm,
    branch_owner_hbm,
    root_len_hbm,
    branch_len_hbm,
    leaf_len_hbm,
    w_query,
    w_keyval,
    w_output,
    node_hbm,
    leaf_hbm,
    mixed,
    entry,
    hidden,
    gain,
    freq,
    leaf_branch,
    branch_root,
    root_owner,
    branch_owner,
    root_len,
    branch_len,
    leaf_len,
    wq,
    wkv,
    wo,
    node,
    leaf,
    q_all,
    part_out,
    part_in,
    term_out,
    term_in,
    load_sem,
    q_send,
    q_recv,
    p_send,
    p_recv,
    t_send,
    t_recv,
):
    me = lax.axis_index("request")
    mine = lax.axis_index("tensor")
    rows, width = hidden.shape
    head_dim = LANES // 2
    chunks = wq.shape[1] // LANES
    body_rows = chunks * rows
    factor = head_dim ** (-0.5)
    splits = 4
    depth = width // splits
    cols = wo.shape[2]

    loads = []

    def load(src, dst):
        copy = pltpu.make_async_copy(src, dst, load_sem.at[len(loads)])
        copy.start()
        loads.append(copy)
        return copy

    index_loads = [
        load(leaf_branch_hbm, leaf_branch),
        load(branch_root_hbm, branch_root),
        load(root_len_hbm, root_len),
        load(branch_len_hbm, branch_len),
        load(leaf_len_hbm, leaf_len),
        load(root_owner_hbm, root_owner),
        load(branch_owner_hbm, branch_owner),
        load(freq_hbm, freq),
    ]
    row_loads = [load(hidden_hbm, hidden), load(gain_hbm, gain)]
    q_loads = []
    for s in range(splits):
        part = pl.ds(s * depth, depth)
        q_loads.append(
            (load(w_query.at[part], wq.at[part]), load(w_keyval.at[part], wkv.at[part]))
        )
    node_load = load(node_hbm, node)
    leaf_load = load(leaf_hbm, leaf)
    o_loads = []
    for k in range(nt):
        target = lax.rem(mine + k, nt)
        o_loads.append(
            load(w_output.at[:, pl.ds(pl.multiple_of(target * cols, cols), cols)], wo.at[k])
        )

    barrier = pltpu.get_barrier_semaphore()

    def greet(k):
        pl.semaphore_signal(
            barrier, inc=1, device_id=(mine, lax.rem(me + k, n)), device_id_type=MESH
        )

    each(1, n, greet)
    for k in range(1, nt):
        pl.semaphore_signal(
            barrier, inc=1, device_id=(lax.rem(mine + k, nt), me), device_id_type=MESH
        )

    for copy in index_loads:
        copy.wait()
    row8 = lax.broadcasted_iota(jnp.int32, (rows, LANES), 0)
    lane8 = lax.broadcasted_iota(jnp.int32, (rows, LANES), 1)
    low8 = lane8 < head_dim
    position = jnp.zeros((rows, LANES), jnp.int32)
    lengths = jnp.zeros((rows, LANES), jnp.int32)
    root_slot, branch_slot = [], []
    for l in range(rows):
        b = leaf_branch[me * rows + l]
        r = branch_root[b]
        own = leaf_len[l]
        position = jnp.where(row8 == l, root_len[r] + branch_len[b] + own, position)
        lengths = jnp.where(row8 == l, own, lengths)
        root_slot.append(lax.rem(root_owner[r] - me + n, n))
        branch_slot.append(lax.rem(branch_owner[b] - me + n, n))
    my_length = jnp.int32(0)
    for owner, length in ((root_owner, root_len), (branch_owner, branch_len)):
        for j in range(owner.shape[0]):
            my_length = my_length + jnp.where(owner[j] == me, length[j], 0)
    angles = position.astype(F32) * freq[...]
    cosine, sine = jnp.cos(angles), jnp.sin(angles)
    first_half = lax.rem(lane8, head_dim) < head_dim // 2

    def rotate(x):
        up = pltpu.roll(x, LANES - head_dim // 2, 1)
        down = pltpu.roll(x, head_dim // 2, 1)
        return x * cosine + jnp.where(first_half, -up, down) * sine

    for copy in row_loads:
        copy.wait()
    widened = hidden[...].astype(F32)
    mean = jnp.sum(widened * widened, -1, keepdims=True) * (1.0 / width)
    normed = (widened * lax.rsqrt(mean + 1e-05) * gain[...]).astype(BF16)
    raw = jnp.zeros((rows, wq.shape[1]), F32)
    raw_entry = jnp.zeros((rows, LANES), F32)
    for s in range(splits):
        for copy in q_loads[s]:
            copy.wait()
        part = slice(s * depth, (s + 1) * depth)
        raw = raw + dot(normed[:, part], wq[part, :], NN)
        raw_entry = raw_entry + dot(normed[:, part], wkv[part, :], NN)
    queries = jnp.concatenate(
        [rotate(raw[:, c * LANES : (c + 1) * LANES]) * factor for c in range(chunks)], 0
    ).astype(BF16)
    q_all[0] = queries

    pl.semaphore_wait(barrier, n - 1 + nt - 1)

    def q_copy(k):
        return pltpu.make_async_remote_copy(
            src_ref=q_all.at[0],
            dst_ref=q_all.at[k],
            send_sem=q_send.at[k],
            recv_sem=q_recv.at[k],
            device_id=(mine, lax.rem(me + k, n)),
            device_id_type=MESH,
        )

    each(1, n, lambda k: q_copy(k).start())

    entry_new = jnp.where(low8, rotate(raw_entry), raw_entry).astype(BF16)
    entry[...] = entry_new
    new32 = entry_new.astype(F32)
    swapped = pltpu.roll(new32, head_dim, 1)
    new_key = jnp.where(low8, new32, swapped)
    new_value = jnp.where(low8, swapped, new32)

    def split_rows(rows_in):
        wide = rows_in.astype(F32)
        turned = pltpu.roll(wide, head_dim, 1)
        low = lax.broadcasted_iota(jnp.int32, wide.shape, 1) < head_dim
        keys = (jnp.where(low, wide, 0.0).astype(BF16), jnp.where(low, 0.0, turned).astype(BF16))
        values = (jnp.where(low, turned, 0.0).astype(BF16), jnp.where(low, 0.0, wide).astype(BF16))
        return keys, values

    node_load.wait()
    node_keys, node_values = split_rows(node[...])

    leaf_load.wait()
    leaf_keys, leaf_values = split_rows(leaf[...])

    block = min(n, 8)

    def p_copy(k):
        return pltpu.make_async_remote_copy(
            src_ref=part_out.at[k],
            dst_ref=part_in.at[k],
            send_sem=p_send.at[k],
            recv_sem=p_recv.at[k],
            device_id=(mine, lax.rem(me - k + n, n)),
            device_id_type=MESH,
        )

    held = lax.broadcasted_iota(jnp.int32, (block * body_rows, node.shape[0]), 1) < my_length

    def owner_block(first):
        rows_query = q_all[pl.ds(first, block)].reshape(block * body_rows, LANES)
        summed = None
        peaks, totals = [], []
        for e in range(2):
            scores = jnp.where(held, dot(rows_query, node_keys[e], NT), FLOOR)
            peak = jnp.max(scores, -1, keepdims=True)
            weights = jnp.exp(scores - peak).astype(BF16)
            peaks.append(peak)
            totals.append(jnp.sum(weights.astype(F32), -1, keepdims=True))
            term = dot(weights, node_values[e], NN)
            summed = term if summed is None else summed + term
        for j in range(block):
            stats = jnp.zeros((rows, LANES), F32)
            for c in range(chunks):
                at = j * body_rows + c * rows
                for e in range(2):
                    lane = 2 * c + e
                    stats = jnp.where(lane8 == lane, peaks[e][at : at + rows], stats)
                    stats = jnp.where(lane8 == 2 * chunks + lane, totals[e][at : at + rows], stats)
            high = stats.astype(BF16).astype(F32)
            middle = (stats - high).astype(BF16).astype(F32)
            small = (stats - high) - middle
            part_out[first + j] = jnp.concatenate(
                [
                    summed[j * body_rows : (j + 1) * body_rows],
                    jnp.where(low8, high, pltpu.roll(small, head_dim, 1)),
                    middle,
                ],
                0,
            ).astype(BF16)

    each(1, n, lambda k: q_copy(k).wait_recv())
    for first in range(0, n, block):
        if n == block:
            owner_block(0)
        elif first == 0:
            lax.fori_loop(
                0,
                n // block,
                lambda i, carry: (owner_block(i * block), carry)[1],
                0,
            )
    each(1, n, lambda k: p_copy(k).start())
    part_in[0] = part_out[0]

    per_leaf = leaf.shape[0] // rows
    column = lax.broadcasted_iota(jnp.int32, (rows, leaf.shape[0]), 1)
    start = lax.broadcasted_iota(jnp.int32, (rows, leaf.shape[0]), 0) * per_leaf
    usable = (column >= start) & (column < start + lengths[:, :1])
    q32 = queries.astype(F32)
    leaf_stats = [jnp.zeros((rows, LANES), F32), jnp.zeros((rows, LANES), F32)]
    leaf_scores = [dot(queries, keys, NT) for keys in leaf_keys]
    leaf_weights = [[], []]
    fresh = []
    for c in range(chunks):
        part = slice(c * rows, (c + 1) * rows)
        product = q32[part] * new_key
        pair = []
        for e in range(2):
            score = jnp.sum(jnp.where(low8 if e == 0 else ~low8, product, 0.0), -1, keepdims=True)
            scores = jnp.where(usable, leaf_scores[e][part], FLOOR)
            peak = jnp.maximum(jnp.max(scores, -1, keepdims=True), score)
            weights = jnp.exp(scores - peak).astype(BF16).astype(F32)
            weight = jnp.exp(score - peak).astype(BF16).astype(F32)
            total = jnp.sum(weights, -1, keepdims=True) + weight
            leaf_weights[e].append(weights)
            pair.append(weight)
            here = lane8 == 2 * c + e
            leaf_stats[0] = jnp.where(here, peak, leaf_stats[0])
            leaf_stats[1] = jnp.where(here, total, leaf_stats[1])
        fresh.append(jnp.where(low8, pair[0], pair[1]) * new_value)
    leaf_sum = jnp.concatenate(fresh, 0)
    for e in range(2):
        leaf_sum = leaf_sum + dot(
            jnp.concatenate(leaf_weights[e], 0).astype(BF16), leaf_values[e], NN
        )

    each(1, n, lambda k: p_copy(k).wait_recv())

    row_of = lax.rem(lax.broadcasted_iota(jnp.int32, part_in.shape[1:], 0), rows)

    def pick(slots):
        chosen = part_in[slots[0]].astype(F32)
        for l in range(1, rows):
            chosen = jnp.where(row_of == l, part_in[slots[l]].astype(F32), chosen)
        high = chosen[body_rows : body_rows + rows]
        stats = (high + chosen[body_rows + rows :]) + pltpu.roll(high, head_dim, 1)
        return chosen[:body_rows], stats, pltpu.roll(stats, LANES - 2 * chunks, 1)

    parts = [pick(root_slot), pick(branch_slot), (leaf_sum, leaf_stats[0], leaf_stats[1])]
    top = jnp.maximum(jnp.maximum(parts[0][1], parts[1][1]), parts[2][1])
    scales = [jnp.exp(p[1] - top) for p in parts]
    bottom = scales[0] * parts[0][2] + scales[1] * parts[1][2] + scales[2] * parts[2][2]
    scales = [s / bottom for s in scales]
    attended = []
    for c in range(chunks):
        part = slice(c * rows, (c + 1) * rows)
        total = None
        for p, s in zip(parts, scales):
            spread = jnp.where(low8, s[:, 2 * c : 2 * c + 1], s[:, 2 * c + 1 : 2 * c + 2])
            term = spread * p[0][part]
            total = term if total is None else total + term
        attended.append(total)
    attended = jnp.concatenate(attended, 1).astype(BF16)

    def t_copy(k):
        return pltpu.make_async_remote_copy(
            src_ref=term_out.at[k],
            dst_ref=term_in.at[k],
            send_sem=t_send.at[k],
            recv_sem=t_recv.at[k],
            device_id=(lax.rem(mine + k, nt), me),
            device_id_type=MESH,
        )

    out_chunks = cols // LANES
    own_term = None
    for k in [*range(1, nt), 0]:
        o_loads[k].wait()
        term = dot(attended, wo[k], NN)
        if k == 0:
            own_term = term
        else:
            term_out[k] = jnp.concatenate(
                [term[:, c * LANES : (c + 1) * LANES] for c in range(out_chunks)], 0
            ).astype(BF16)
            t_copy(k).start()
    for k in range(1, nt):
        t_copy(k).wait_recv()
    for c in range(out_chunks):
        part = slice(c * LANES, (c + 1) * LANES)
        total = own_term[:, part]
        for k in range(1, nt):
            total = total + term_in[k].astype(F32)[c * rows : (c + 1) * rows]
        mixed[:, part] = total.astype(BF16)

    each(1, n, lambda k: q_copy(k).wait_send())
    each(1, n, lambda k: p_copy(k).wait_send())
    for k in range(1, nt):
        t_copy(k).wait_send()


def deliver(mixed, entry, mixed_out, entry_out, sem):
    first = pltpu.make_async_copy(mixed, mixed_out, sem.at[0])
    second = pltpu.make_async_copy(entry, entry_out, sem.at[1])
    first.start()
    second.start()
    first.wait()
    second.wait()


def local(
    n,
    nt,
    hidden,
    norm_gain,
    w_query,
    w_keyval,
    w_output,
    node_cache,
    leaf_cache,
    leaf_branch,
    branch_root,
    root_owner,
    branch_owner,
    root_len,
    branch_len,
    leaf_len,
):
    rows, width = hidden.shape
    head_dim = w_keyval.shape[1] // 2
    inner = w_query.shape[1]
    cols = w_output.shape[1] // nt
    power = (np.arange(LANES) % (head_dim // 2)) * 2.0 / head_dim
    freq = jnp.asarray((10000.0 ** (-power)).astype(np.float32)[None, :])
    node = node_cache.reshape(-1, LANES)
    leaf = leaf_cache.reshape(-1, LANES)
    body_rows = inner // LANES * rows
    dma = pltpu.SemaphoreType.DMA
    shapes = (
        jax.ShapeDtypeStruct((rows, cols), BF16),
        jax.ShapeDtypeStruct((rows, LANES), BF16),
    )
    operands = (
        hidden,
        norm_gain[None, :],
        freq,
        leaf_branch,
        branch_root,
        root_owner,
        branch_owner,
        root_len,
        branch_len,
        leaf_len,
        w_query,
        w_keyval,
        w_output,
        node,
        leaf,
    )
    mixed, entry = pl.pallas_call(
        functools.partial(kernel, n, nt),
        out_shape=shapes,
        in_specs=[pl.BlockSpec(memory_space=pltpu.HBM)] * len(operands),
        out_specs=(pl.BlockSpec(memory_space=pltpu.VMEM),) * 2,
        scratch_shapes=[
            *[pltpu.VMEM(a.shape, a.dtype) for a in operands[:3]],
            *[pltpu.SMEM(a.shape, a.dtype) for a in operands[3:10]],
            pltpu.VMEM(w_query.shape, BF16),
            pltpu.VMEM(w_keyval.shape, BF16),
            pltpu.VMEM((nt, inner, cols), BF16),
            pltpu.VMEM(node.shape, BF16),
            pltpu.VMEM(leaf.shape, BF16),
            pltpu.VMEM((n, body_rows, LANES), BF16),
            pltpu.VMEM((n, body_rows + 2 * rows, LANES), BF16),
            pltpu.VMEM((n, body_rows + 2 * rows, LANES), BF16),
            pltpu.VMEM((nt, cols // LANES * rows, LANES), BF16),
            pltpu.VMEM((nt, cols // LANES * rows, LANES), BF16),
            dma((10 + 8 + 2 + nt,)),
            dma((n,)),
            dma((n,)),
            dma((n,)),
            dma((n,)),
            dma((nt,)),
            dma((nt,)),
        ],
        compiler_params=pltpu.CompilerParams(
            collective_id=0, has_side_effects=True, vmem_limit_bytes=63 * 1024 * 1024
        ),
    )(*operands)
    anywhere = pl.BlockSpec(memory_space=pl.ANY)
    mixed, entry = pl.pallas_call(
        deliver,
        out_shape=shapes,
        in_specs=[anywhere] * 2,
        out_specs=(anywhere,) * 2,
        scratch_shapes=[dma((2,))],
        compiler_params=pltpu.CompilerParams(vmem_limit_bytes=63 * 1024 * 1024),
    )(mixed, entry)
    return (mixed, entry[:, None, :])


def solution(mesh):
    in_specs = (
        P("request", None),
        P(),
        P(None, "tensor"),
        P(None, "tensor"),
        P("tensor", None),
        P("request", "tensor", None, None),
        P("request", "tensor", None, None),
        P(),
        P(),
        P(),
        P(),
        P(),
        P(),
        P("request"),
    )
    out_specs = (P("request", "tensor"), P("request", "tensor", None))
    run = functools.partial(local, mesh.shape["request"], mesh.shape["tensor"])
    return jax.shard_map(run, mesh=mesh, in_specs=in_specs, out_specs=out_specs, check_vma=False)
```

```python
import functools

import jax
import jax.numpy as jnp
import numpy as np
from jax import lax
from jax.experimental import pallas as pl
from jax.experimental.pallas import tpu as pltpu
from jax.sharding import PartitionSpec as P

FLOOR = -1e30
MESH = pl.DeviceIdType.MESH
F32 = jnp.float32
BF16 = jnp.bfloat16
LANES = 128
NT = (((1,), (1,)), ((), ()))
NN = (((1,), (0,)), ((), ()))


def each(low, high, step):
    if high - low <= 8:
        for k in range(low, high):
            step(k)
    else:
        lax.fori_loop(low, high, lambda k, carry: (step(k), carry)[1], 0)


def dot(a, b, dims):
    return lax.dot_general(a, b, dims, preferred_element_type=F32)


def kernel(
    n,
    nt,
    hidden_hbm,
    gain_hbm,
    freq_hbm,
    leaf_branch_hbm,
    branch_root_hbm,
    root_owner_hbm,
    branch_owner_hbm,
    root_len_hbm,
    branch_len_hbm,
    leaf_len_hbm,
    w_query,
    w_keyval,
    w_output,
    node_hbm,
    leaf_hbm,
    mixed,
    entry,
    hidden,
    gain,
    freq,
    leaf_branch,
    branch_root,
    root_owner,
    branch_owner,
    root_len,
    branch_len,
    leaf_len,
    wq,
    wkv,
    wo,
    node,
    leaf,
    q_all,
    part_out,
    part_in,
    term_out,
    term_in,
    load_sem,
    q_send,
    q_recv,
    p_send,
    p_recv,
    t_send,
    t_recv,
):
    me = lax.axis_index("request")
    mine = lax.axis_index("tensor")
    rows, width = hidden.shape
    head_dim = LANES // 2
    chunks = wq.shape[1] // LANES
    body_rows = chunks * rows
    factor = head_dim ** (-0.5)
    splits = 4
    depth = width // splits
    cols = wo.shape[2]

    loads = []

    def load(src, dst):
        copy = pltpu.make_async_copy(src, dst, load_sem.at[len(loads)])
        copy.start()
        loads.append(copy)
        return copy

    index_loads = [
        load(leaf_branch_hbm, leaf_branch),
        load(branch_root_hbm, branch_root),
        load(root_len_hbm, root_len),
        load(branch_len_hbm, branch_len),
        load(leaf_len_hbm, leaf_len),
        load(root_owner_hbm, root_owner),
        load(branch_owner_hbm, branch_owner),
        load(freq_hbm, freq),
    ]
    row_loads = [load(hidden_hbm, hidden), load(gain_hbm, gain)]
    q_loads = []
    for s in range(splits):
        part = pl.ds(s * depth, depth)
        q_loads.append(
            (load(w_query.at[part], wq.at[part]), load(w_keyval.at[part], wkv.at[part]))
        )
    node_load = load(node_hbm, node)
    leaf_load = load(leaf_hbm, leaf)

    barrier = pltpu.get_barrier_semaphore()

    def greet(k):
        pl.semaphore_signal(
            barrier, inc=1, device_id=(mine, lax.rem(me + k, n)), device_id_type=MESH
        )

    each(1, n, greet)
    for k in range(1, nt):
        pl.semaphore_signal(
            barrier, inc=1, device_id=(lax.rem(mine + k, nt), me), device_id_type=MESH
        )

    for copy in index_loads:
        copy.wait()
    row8 = lax.broadcasted_iota(jnp.int32, (rows, LANES), 0)
    lane8 = lax.broadcasted_iota(jnp.int32, (rows, LANES), 1)
    low8 = lane8 < head_dim
    position = jnp.zeros((rows, LANES), jnp.int32)
    lengths = jnp.zeros((rows, LANES), jnp.int32)
    root_slot, branch_slot = [], []
    for l in range(rows):
        b = leaf_branch[me * rows + l]
        r = branch_root[b]
        own = leaf_len[l]
        position = jnp.where(row8 == l, root_len[r] + branch_len[b] + own, position)
        lengths = jnp.where(row8 == l, own, lengths)
        root_slot.append(lax.rem(root_owner[r] - me + n, n))
        branch_slot.append(lax.rem(branch_owner[b] - me + n, n))
    my_length = jnp.int32(0)
    for owner, length in ((root_owner, root_len), (branch_owner, branch_len)):
        for j in range(owner.shape[0]):
            my_length = my_length + jnp.where(owner[j] == me, length[j], 0)
    angles = position.astype(F32) * freq[...]
    cosine, sine = jnp.cos(angles), jnp.sin(angles)
    first_half = lax.rem(lane8, head_dim) < head_dim // 2

    def rotate(x):
        up = pltpu.roll(x, LANES - head_dim // 2, 1)
        down = pltpu.roll(x, head_dim // 2, 1)
        return x * cosine + jnp.where(first_half, -up, down) * sine

    for copy in row_loads:
        copy.wait()
    widened = hidden[...].astype(F32)
    mean = jnp.sum(widened * widened, -1, keepdims=True) * (1.0 / width)
    normed = (widened * lax.rsqrt(mean + 1e-05) * gain[...]).astype(BF16)
    raw = jnp.zeros((rows, wq.shape[1]), F32)
    raw_entry = jnp.zeros((rows, LANES), F32)
    for s in range(splits):
        for copy in q_loads[s]:
            copy.wait()
        part = slice(s * depth, (s + 1) * depth)
        raw = raw + dot(normed[:, part], wq[part, :], NN)
        raw_entry = raw_entry + dot(normed[:, part], wkv[part, :], NN)
    queries = jnp.concatenate(
        [rotate(raw[:, c * LANES : (c + 1) * LANES]) * factor for c in range(chunks)], 0
    ).astype(BF16)
    q_all[0] = queries

    pl.semaphore_wait(barrier, n - 1 + nt - 1)

    def q_copy(k):
        return pltpu.make_async_remote_copy(
            src_ref=q_all.at[0],
            dst_ref=q_all.at[k],
            send_sem=q_send.at[k],
            recv_sem=q_recv.at[k],
            device_id=(mine, lax.rem(me + k, n)),
            device_id_type=MESH,
        )

    each(1, n, lambda k: q_copy(k).start())

    o_loads = []
    for k in range(nt):
        target = lax.rem(mine + k, nt)
        o_loads.append(
            load(w_output.at[:, pl.ds(pl.multiple_of(target * cols, cols), cols)], wo.at[k])
        )

    entry_new = jnp.where(low8, rotate(raw_entry), raw_entry).astype(BF16)
    entry[...] = entry_new
    new32 = entry_new.astype(F32)
    swapped = pltpu.roll(new32, head_dim, 1)
    new_key = jnp.where(low8, new32, swapped)
    new_value = jnp.where(low8, swapped, new32)

    def split_rows(rows_in):
        wide = rows_in.astype(F32)
        turned = pltpu.roll(wide, head_dim, 1)
        low = lax.broadcasted_iota(jnp.int32, wide.shape, 1) < head_dim
        keys = (jnp.where(low, wide, 0.0).astype(BF16), jnp.where(low, 0.0, turned).astype(BF16))
        values = (jnp.where(low, turned, 0.0).astype(BF16), jnp.where(low, 0.0, wide).astype(BF16))
        return keys, values

    node_load.wait()
    node_keys, node_values = split_rows(node[...])

    leaf_load.wait()
    leaf_keys, leaf_values = split_rows(leaf[...])

    block = 4 if n == 8 else min(n, 8)

    def p_copy(k):
        return pltpu.make_async_remote_copy(
            src_ref=part_out.at[k],
            dst_ref=part_in.at[k],
            send_sem=p_send.at[k],
            recv_sem=p_recv.at[k],
            device_id=(mine, lax.rem(me - k + n, n)),
            device_id_type=MESH,
        )

    held = lax.broadcasted_iota(jnp.int32, (block * body_rows, node.shape[0]), 1) < my_length

    def owner_block(first):
        rows_query = q_all[pl.ds(first, block)].reshape(block * body_rows, LANES)
        summed = None
        peaks, totals = [], []
        for e in range(2):
            scores = jnp.where(held, dot(rows_query, node_keys[e], NT), FLOOR)
            peak = jnp.max(scores, -1, keepdims=True)
            weights = jnp.exp(scores - peak).astype(BF16)
            peaks.append(peak)
            totals.append(jnp.sum(weights.astype(F32), -1, keepdims=True))
            term = dot(weights, node_values[e], NN)
            summed = term if summed is None else summed + term
        for j in range(block):
            stats = jnp.zeros((rows, LANES), F32)
            for c in range(chunks):
                at = j * body_rows + c * rows
                for e in range(2):
                    lane = 2 * c + e
                    stats = jnp.where(lane8 == lane, peaks[e][at : at + rows], stats)
                    stats = jnp.where(lane8 == 2 * chunks + lane, totals[e][at : at + rows], stats)
            high = stats.astype(BF16).astype(F32)
            middle = (stats - high).astype(BF16).astype(F32)
            small = (stats - high) - middle
            part_out[first + j] = jnp.concatenate(
                [
                    summed[j * body_rows : (j + 1) * body_rows],
                    jnp.where(low8, high, pltpu.roll(small, head_dim, 1)),
                    middle,
                ],
                0,
            ).astype(BF16)

    if n <= 2 * block:
        for first in range(0, n, block):
            each(max(first, 1), first + block, lambda k: q_copy(k).wait_recv())
            owner_block(first)
            each(max(first, 1), first + block, lambda k: p_copy(k).start())
    else:
        each(1, n, lambda k: q_copy(k).wait_recv())
        lax.fori_loop(
            0, n // block, lambda i, carry: (owner_block(i * block), carry)[1], 0
        )
        each(1, n, lambda k: p_copy(k).start())
    part_in[0] = part_out[0]

    per_leaf = leaf.shape[0] // rows
    column = lax.broadcasted_iota(jnp.int32, (rows, leaf.shape[0]), 1)
    start = lax.broadcasted_iota(jnp.int32, (rows, leaf.shape[0]), 0) * per_leaf
    usable = (column >= start) & (column < start + lengths[:, :1])
    q32 = queries.astype(F32)
    leaf_stats = [jnp.zeros((rows, LANES), F32), jnp.zeros((rows, LANES), F32)]
    leaf_scores = [dot(queries, keys, NT) for keys in leaf_keys]
    leaf_weights = [[], []]
    fresh = []
    for c in range(chunks):
        part = slice(c * rows, (c + 1) * rows)
        product = q32[part] * new_key
        pair = []
        for e in range(2):
            score = jnp.sum(jnp.where(low8 if e == 0 else ~low8, product, 0.0), -1, keepdims=True)
            scores = jnp.where(usable, leaf_scores[e][part], FLOOR)
            peak = jnp.maximum(jnp.max(scores, -1, keepdims=True), score)
            weights = jnp.exp(scores - peak).astype(BF16).astype(F32)
            weight = jnp.exp(score - peak).astype(BF16).astype(F32)
            total = jnp.sum(weights, -1, keepdims=True) + weight
            leaf_weights[e].append(weights)
            pair.append(weight)
            here = lane8 == 2 * c + e
            leaf_stats[0] = jnp.where(here, peak, leaf_stats[0])
            leaf_stats[1] = jnp.where(here, total, leaf_stats[1])
        fresh.append(jnp.where(low8, pair[0], pair[1]) * new_value)
    leaf_sum = jnp.concatenate(fresh, 0)
    for e in range(2):
        leaf_sum = leaf_sum + dot(
            jnp.concatenate(leaf_weights[e], 0).astype(BF16), leaf_values[e], NN
        )

    each(1, n, lambda k: p_copy(k).wait_recv())

    row_of = lax.rem(lax.broadcasted_iota(jnp.int32, part_in.shape[1:], 0), rows)

    def pick(slots):
        chosen = part_in[slots[0]].astype(F32)
        for l in range(1, rows):
            chosen = jnp.where(row_of == l, part_in[slots[l]].astype(F32), chosen)
        high = chosen[body_rows : body_rows + rows]
        stats = (high + chosen[body_rows + rows :]) + pltpu.roll(high, head_dim, 1)
        return chosen[:body_rows], stats, pltpu.roll(stats, LANES - 2 * chunks, 1)

    parts = [pick(root_slot), pick(branch_slot), (leaf_sum, leaf_stats[0], leaf_stats[1])]
    top = jnp.maximum(jnp.maximum(parts[0][1], parts[1][1]), parts[2][1])
    scales = [jnp.exp(p[1] - top) for p in parts]
    bottom = scales[0] * parts[0][2] + scales[1] * parts[1][2] + scales[2] * parts[2][2]
    scales = [s / bottom for s in scales]
    attended = []
    for c in range(chunks):
        part = slice(c * rows, (c + 1) * rows)
        total = None
        for p, s in zip(parts, scales):
            spread = jnp.where(low8, s[:, 2 * c : 2 * c + 1], s[:, 2 * c + 1 : 2 * c + 2])
            term = spread * p[0][part]
            total = term if total is None else total + term
        attended.append(total)
    attended = jnp.concatenate(attended, 1).astype(BF16)

    def t_copy(k):
        return pltpu.make_async_remote_copy(
            src_ref=term_out.at[k],
            dst_ref=term_in.at[k],
            send_sem=t_send.at[k],
            recv_sem=t_recv.at[k],
            device_id=(lax.rem(mine + k, nt), me),
            device_id_type=MESH,
        )

    out_chunks = cols // LANES
    own_term = None
    for k in [*range(1, nt), 0]:
        o_loads[k].wait()
        term = dot(attended, wo[k], NN)
        if k == 0:
            own_term = term
        else:
            term_out[k] = jnp.concatenate(
                [term[:, c * LANES : (c + 1) * LANES] for c in range(out_chunks)], 0
            ).astype(BF16)
            t_copy(k).start()
    for k in range(1, nt):
        t_copy(k).wait_recv()
    for c in range(out_chunks):
        part = slice(c * LANES, (c + 1) * LANES)
        total = own_term[:, part]
        for k in range(1, nt):
            total = total + term_in[k].astype(F32)[c * rows : (c + 1) * rows]
        mixed[:, part] = total.astype(BF16)

    each(1, n, lambda k: q_copy(k).wait_send())
    each(1, n, lambda k: p_copy(k).wait_send())
    for k in range(1, nt):
        t_copy(k).wait_send()


def deliver(mixed, entry, mixed_out, entry_out, sem):
    first = pltpu.make_async_copy(mixed, mixed_out, sem.at[0])
    second = pltpu.make_async_copy(entry, entry_out, sem.at[1])
    first.start()
    second.start()
    first.wait()
    second.wait()


def local(
    n,
    nt,
    hidden,
    norm_gain,
    w_query,
    w_keyval,
    w_output,
    node_cache,
    leaf_cache,
    leaf_branch,
    branch_root,
    root_owner,
    branch_owner,
    root_len,
    branch_len,
    leaf_len,
):
    rows, width = hidden.shape
    head_dim = w_keyval.shape[1] // 2
    inner = w_query.shape[1]
    cols = w_output.shape[1] // nt
    power = (np.arange(LANES) % (head_dim // 2)) * 2.0 / head_dim
    freq = jnp.asarray((10000.0 ** (-power)).astype(np.float32)[None, :])
    node = node_cache.reshape(-1, LANES)
    leaf = leaf_cache.reshape(-1, LANES)
    body_rows = inner // LANES * rows
    dma = pltpu.SemaphoreType.DMA
    shapes = (
        jax.ShapeDtypeStruct((rows, cols), BF16),
        jax.ShapeDtypeStruct((rows, LANES), BF16),
    )
    operands = (
        hidden,
        norm_gain[None, :],
        freq,
        leaf_branch,
        branch_root,
        root_owner,
        branch_owner,
        root_len,
        branch_len,
        leaf_len,
        w_query,
        w_keyval,
        w_output,
        node,
        leaf,
    )
    mixed, entry = pl.pallas_call(
        functools.partial(kernel, n, nt),
        out_shape=shapes,
        in_specs=[pl.BlockSpec(memory_space=pltpu.HBM)] * len(operands),
        out_specs=(pl.BlockSpec(memory_space=pltpu.VMEM),) * 2,
        scratch_shapes=[
            *[pltpu.VMEM(a.shape, a.dtype) for a in operands[:3]],
            *[pltpu.SMEM(a.shape, a.dtype) for a in operands[3:10]],
            pltpu.VMEM(w_query.shape, BF16),
            pltpu.VMEM(w_keyval.shape, BF16),
            pltpu.VMEM((nt, inner, cols), BF16),
            pltpu.VMEM(node.shape, BF16),
            pltpu.VMEM(leaf.shape, BF16),
            pltpu.VMEM((n, body_rows, LANES), BF16),
            pltpu.VMEM((n, body_rows + 2 * rows, LANES), BF16),
            pltpu.VMEM((n, body_rows + 2 * rows, LANES), BF16),
            pltpu.VMEM((nt, cols // LANES * rows, LANES), BF16),
            pltpu.VMEM((nt, cols // LANES * rows, LANES), BF16),
            dma((10 + 8 + 2 + nt,)),
            dma((n,)),
            dma((n,)),
            dma((n,)),
            dma((n,)),
            dma((nt,)),
            dma((nt,)),
        ],
        compiler_params=pltpu.CompilerParams(
            collective_id=0, has_side_effects=True, vmem_limit_bytes=63 * 1024 * 1024
        ),
    )(*operands)
    anywhere = pl.BlockSpec(memory_space=pl.ANY)
    mixed, entry = pl.pallas_call(
        deliver,
        out_shape=shapes,
        in_specs=[anywhere] * 2,
        out_specs=(anywhere,) * 2,
        scratch_shapes=[dma((2,))],
        compiler_params=pltpu.CompilerParams(vmem_limit_bytes=63 * 1024 * 1024),
    )(mixed, entry)
    return (mixed, entry[:, None, :])


def solution(mesh):
    in_specs = (
        P("request", None),
        P(),
        P(None, "tensor"),
        P(None, "tensor"),
        P("tensor", None),
        P("request", "tensor", None, None),
        P("request", "tensor", None, None),
        P(),
        P(),
        P(),
        P(),
        P(),
        P(),
        P("request"),
    )
    out_specs = (P("request", "tensor"), P("request", "tensor", None))
    run = functools.partial(local, mesh.shape["request"], mesh.shape["tensor"])
    return jax.shard_map(run, mesh=mesh, in_specs=in_specs, out_specs=out_specs, check_vma=False)
```

```python
import functools

import jax
import jax.numpy as jnp
import numpy as np
from jax import lax
from jax.experimental import pallas as pl
from jax.experimental.pallas import tpu as pltpu
from jax.sharding import PartitionSpec as P

FLOOR = -1e30
MESH = pl.DeviceIdType.MESH
F32 = jnp.float32
BF16 = jnp.bfloat16
LANES = 128
NT = (((1,), (1,)), ((), ()))
NN = (((1,), (0,)), ((), ()))


def each(low, high, step):
    if high - low <= 8:
        for k in range(low, high):
            step(k)
    else:
        lax.fori_loop(low, high, lambda k, carry: (step(k), carry)[1], 0)


def dot(a, b, dims):
    return lax.dot_general(a, b, dims, preferred_element_type=F32)


def kernel(
    n,
    nt,
    hidden_hbm,
    gain_hbm,
    freq_hbm,
    leaf_branch_hbm,
    branch_root_hbm,
    root_owner_hbm,
    branch_owner_hbm,
    root_len_hbm,
    branch_len_hbm,
    leaf_len_hbm,
    w_query,
    w_keyval,
    w_output,
    node_hbm,
    leaf_hbm,
    mixed,
    entry,
    hidden,
    gain,
    freq,
    leaf_branch,
    branch_root,
    root_owner,
    branch_owner,
    root_len,
    branch_len,
    leaf_len,
    wq,
    wkv,
    wo,
    node,
    leaf,
    q_all,
    part_out,
    part_in,
    term_out,
    term_in,
    load_sem,
    q_send,
    q_recv,
    p_send,
    p_recv,
    t_send,
    t_recv,
):
    me = lax.axis_index("request")
    mine = lax.axis_index("tensor")
    rows, width = hidden.shape
    head_dim = LANES // 2
    chunks = wq.shape[1] // LANES
    body_rows = chunks * rows
    factor = head_dim ** (-0.5)
    splits = 4
    depth = width // splits
    cols = wo.shape[2]

    loads = []

    def load(src, dst):
        copy = pltpu.make_async_copy(src, dst, load_sem.at[len(loads)])
        copy.start()
        loads.append(copy)
        return copy

    index_loads = [
        load(leaf_branch_hbm, leaf_branch),
        load(branch_root_hbm, branch_root),
        load(root_len_hbm, root_len),
        load(branch_len_hbm, branch_len),
        load(leaf_len_hbm, leaf_len),
        load(root_owner_hbm, root_owner),
        load(branch_owner_hbm, branch_owner),
        load(freq_hbm, freq),
    ]
    row_loads = [load(hidden_hbm, hidden), load(gain_hbm, gain)]
    q_loads = []
    for s in range(splits):
        part = pl.ds(s * depth, depth)
        q_loads.append(load(w_query.at[part], wq.at[part]))
    entry_load = load(w_keyval, wkv)
    node_load = load(node_hbm, node)
    leaf_load = load(leaf_hbm, leaf)

    barrier = pltpu.get_barrier_semaphore()

    def greet(k):
        pl.semaphore_signal(
            barrier, inc=1, device_id=(mine, lax.rem(me + k, n)), device_id_type=MESH
        )

    each(1, n, greet)
    for k in range(1, nt):
        pl.semaphore_signal(
            barrier, inc=1, device_id=(lax.rem(mine + k, nt), me), device_id_type=MESH
        )

    for copy in index_loads:
        copy.wait()
    row8 = lax.broadcasted_iota(jnp.int32, (rows, LANES), 0)
    lane8 = lax.broadcasted_iota(jnp.int32, (rows, LANES), 1)
    low8 = lane8 < head_dim
    position = jnp.zeros((rows, LANES), jnp.int32)
    lengths = jnp.zeros((rows, LANES), jnp.int32)
    root_slot, branch_slot = [], []
    for l in range(rows):
        b = leaf_branch[me * rows + l]
        r = branch_root[b]
        own = leaf_len[l]
        position = jnp.where(row8 == l, root_len[r] + branch_len[b] + own, position)
        lengths = jnp.where(row8 == l, own, lengths)
        root_slot.append(lax.rem(root_owner[r] - me + n, n))
        branch_slot.append(lax.rem(branch_owner[b] - me + n, n))
    my_length = jnp.int32(0)
    for owner, length in ((root_owner, root_len), (branch_owner, branch_len)):
        for j in range(owner.shape[0]):
            my_length = my_length + jnp.where(owner[j] == me, length[j], 0)
    angles = position.astype(F32) * freq[...]
    cosine, sine = jnp.cos(angles), jnp.sin(angles)
    first_half = lax.rem(lane8, head_dim) < head_dim // 2

    def rotate(x):
        up = pltpu.roll(x, LANES - head_dim // 2, 1)
        down = pltpu.roll(x, head_dim // 2, 1)
        return x * cosine + jnp.where(first_half, -up, down) * sine

    for copy in row_loads:
        copy.wait()
    widened = hidden[...].astype(F32)
    mean = jnp.sum(widened * widened, -1, keepdims=True) * (1.0 / width)
    normed = (widened * lax.rsqrt(mean + 1e-05) * gain[...]).astype(BF16)
    raw = jnp.zeros((rows, wq.shape[1]), F32)
    for s in range(splits):
        q_loads[s].wait()
        part = slice(s * depth, (s + 1) * depth)
        raw = raw + dot(normed[:, part], wq[part, :], NN)
    queries = jnp.concatenate(
        [rotate(raw[:, c * LANES : (c + 1) * LANES]) * factor for c in range(chunks)], 0
    ).astype(BF16)
    q_all[0] = queries

    pl.semaphore_wait(barrier, n - 1 + nt - 1)

    def q_copy(k):
        return pltpu.make_async_remote_copy(
            src_ref=q_all.at[0],
            dst_ref=q_all.at[k],
            send_sem=q_send.at[k],
            recv_sem=q_recv.at[k],
            device_id=(mine, lax.rem(me + k, n)),
            device_id_type=MESH,
        )

    each(1, n, lambda k: q_copy(k).start())

    o_loads = []
    for k in range(nt):
        target = lax.rem(mine + k, nt)
        o_loads.append(
            load(w_output.at[:, pl.ds(pl.multiple_of(target * cols, cols), cols)], wo.at[k])
        )

    entry_load.wait()
    raw_entry = dot(normed, wkv[...], NN)
    entry_new = jnp.where(low8, rotate(raw_entry), raw_entry).astype(BF16)
    entry[...] = entry_new
    new32 = entry_new.astype(F32)
    swapped = pltpu.roll(new32, head_dim, 1)
    new_key = jnp.where(low8, new32, swapped)
    new_value = jnp.where(low8, swapped, new32)

    def split_rows(rows_in):
        wide = rows_in.astype(F32)
        turned = pltpu.roll(wide, head_dim, 1)
        low = lax.broadcasted_iota(jnp.int32, wide.shape, 1) < head_dim
        keys = (jnp.where(low, wide, 0.0).astype(BF16), jnp.where(low, 0.0, turned).astype(BF16))
        values = (jnp.where(low, turned, 0.0).astype(BF16), jnp.where(low, 0.0, wide).astype(BF16))
        return keys, values

    node_load.wait()
    node_keys, node_values = split_rows(node[...])

    leaf_load.wait()
    leaf_keys, leaf_values = split_rows(leaf[...])

    block = 4 if n == 8 else min(n, 8)

    def p_copy(k):
        return pltpu.make_async_remote_copy(
            src_ref=part_out.at[k],
            dst_ref=part_in.at[k],
            send_sem=p_send.at[k],
            recv_sem=p_recv.at[k],
            device_id=(mine, lax.rem(me - k + n, n)),
            device_id_type=MESH,
        )

    held = lax.broadcasted_iota(jnp.int32, (block * body_rows, node.shape[0]), 1) < my_length

    def owner_block(first):
        rows_query = q_all[pl.ds(first, block)].reshape(block * body_rows, LANES)
        summed = None
        peaks, totals = [], []
        for e in range(2):
            scores = jnp.where(held, dot(rows_query, node_keys[e], NT), FLOOR)
            peak = jnp.max(scores, -1, keepdims=True)
            weights = jnp.exp(scores - peak).astype(BF16)
            peaks.append(peak)
            totals.append(jnp.sum(weights.astype(F32), -1, keepdims=True))
            term = dot(weights, node_values[e], NN)
            summed = term if summed is None else summed + term
        for j in range(block):
            stats = jnp.zeros((rows, LANES), F32)
            for c in range(chunks):
                at = j * body_rows + c * rows
                for e in range(2):
                    lane = 2 * c + e
                    stats = jnp.where(lane8 == lane, peaks[e][at : at + rows], stats)
                    stats = jnp.where(lane8 == 2 * chunks + lane, totals[e][at : at + rows], stats)
            high = stats.astype(BF16).astype(F32)
            middle = (stats - high).astype(BF16).astype(F32)
            small = (stats - high) - middle
            part_out[first + j] = jnp.concatenate(
                [
                    summed[j * body_rows : (j + 1) * body_rows],
                    jnp.where(low8, high, pltpu.roll(small, head_dim, 1)),
                    middle,
                ],
                0,
            ).astype(BF16)

    if n <= 2 * block:
        for first in range(0, n, block):
            each(max(first, 1), first + block, lambda k: q_copy(k).wait_recv())
            owner_block(first)
            each(max(first, 1), first + block, lambda k: p_copy(k).start())
    else:
        each(1, n, lambda k: q_copy(k).wait_recv())
        lax.fori_loop(
            0, n // block, lambda i, carry: (owner_block(i * block), carry)[1], 0
        )
        each(1, n, lambda k: p_copy(k).start())
    part_in[0] = part_out[0]

    per_leaf = leaf.shape[0] // rows
    column = lax.broadcasted_iota(jnp.int32, (rows, leaf.shape[0]), 1)
    start = lax.broadcasted_iota(jnp.int32, (rows, leaf.shape[0]), 0) * per_leaf
    usable = (column >= start) & (column < start + lengths[:, :1])
    q32 = queries.astype(F32)
    leaf_stats = [jnp.zeros((rows, LANES), F32), jnp.zeros((rows, LANES), F32)]
    leaf_scores = [dot(queries, keys, NT) for keys in leaf_keys]
    leaf_weights = [[], []]
    fresh = []
    for c in range(chunks):
        part = slice(c * rows, (c + 1) * rows)
        product = q32[part] * new_key
        pair = []
        for e in range(2):
            score = jnp.sum(jnp.where(low8 if e == 0 else ~low8, product, 0.0), -1, keepdims=True)
            scores = jnp.where(usable, leaf_scores[e][part], FLOOR)
            peak = jnp.maximum(jnp.max(scores, -1, keepdims=True), score)
            weights = jnp.exp(scores - peak).astype(BF16).astype(F32)
            weight = jnp.exp(score - peak).astype(BF16).astype(F32)
            total = jnp.sum(weights, -1, keepdims=True) + weight
            leaf_weights[e].append(weights)
            pair.append(weight)
            here = lane8 == 2 * c + e
            leaf_stats[0] = jnp.where(here, peak, leaf_stats[0])
            leaf_stats[1] = jnp.where(here, total, leaf_stats[1])
        fresh.append(jnp.where(low8, pair[0], pair[1]) * new_value)
    leaf_sum = jnp.concatenate(fresh, 0)
    for e in range(2):
        leaf_sum = leaf_sum + dot(
            jnp.concatenate(leaf_weights[e], 0).astype(BF16), leaf_values[e], NN
        )

    each(1, n, lambda k: p_copy(k).wait_recv())

    row_of = lax.rem(lax.broadcasted_iota(jnp.int32, part_in.shape[1:], 0), rows)

    def pick(slots):
        chosen = part_in[slots[0]].astype(F32)
        for l in range(1, rows):
            chosen = jnp.where(row_of == l, part_in[slots[l]].astype(F32), chosen)
        high = chosen[body_rows : body_rows + rows]
        stats = (high + chosen[body_rows + rows :]) + pltpu.roll(high, head_dim, 1)
        return chosen[:body_rows], stats, pltpu.roll(stats, LANES - 2 * chunks, 1)

    parts = [pick(root_slot), pick(branch_slot), (leaf_sum, leaf_stats[0], leaf_stats[1])]
    top = jnp.maximum(jnp.maximum(parts[0][1], parts[1][1]), parts[2][1])
    scales = [jnp.exp(p[1] - top) for p in parts]
    bottom = scales[0] * parts[0][2] + scales[1] * parts[1][2] + scales[2] * parts[2][2]
    scales = [s / bottom for s in scales]
    attended = []
    for c in range(chunks):
        part = slice(c * rows, (c + 1) * rows)
        total = None
        for p, s in zip(parts, scales):
            spread = jnp.where(low8, s[:, 2 * c : 2 * c + 1], s[:, 2 * c + 1 : 2 * c + 2])
            term = spread * p[0][part]
            total = term if total is None else total + term
        attended.append(total)
    attended = jnp.concatenate(attended, 1).astype(BF16)

    def t_copy(k):
        return pltpu.make_async_remote_copy(
            src_ref=term_out.at[k],
            dst_ref=term_in.at[k],
            send_sem=t_send.at[k],
            recv_sem=t_recv.at[k],
            device_id=(lax.rem(mine + k, nt), me),
            device_id_type=MESH,
        )

    out_chunks = cols // LANES
    own_term = None
    for k in [*range(1, nt), 0]:
        o_loads[k].wait()
        term = dot(attended, wo[k], NN)
        if k == 0:
            own_term = term
        else:
            term_out[k] = jnp.concatenate(
                [term[:, c * LANES : (c + 1) * LANES] for c in range(out_chunks)], 0
            ).astype(BF16)
            t_copy(k).start()
    for k in range(1, nt):
        t_copy(k).wait_recv()
    for c in range(out_chunks):
        part = slice(c * LANES, (c + 1) * LANES)
        total = own_term[:, part]
        for k in range(1, nt):
            total = total + term_in[k].astype(F32)[c * rows : (c + 1) * rows]
        mixed[:, part] = total.astype(BF16)

    each(1, n, lambda k: q_copy(k).wait_send())
    each(1, n, lambda k: p_copy(k).wait_send())
    for k in range(1, nt):
        t_copy(k).wait_send()


def deliver(mixed, entry, mixed_out, entry_out, sem):
    first = pltpu.make_async_copy(mixed, mixed_out, sem.at[0])
    second = pltpu.make_async_copy(entry, entry_out, sem.at[1])
    first.start()
    second.start()
    first.wait()
    second.wait()


def local(
    n,
    nt,
    hidden,
    norm_gain,
    w_query,
    w_keyval,
    w_output,
    node_cache,
    leaf_cache,
    leaf_branch,
    branch_root,
    root_owner,
    branch_owner,
    root_len,
    branch_len,
    leaf_len,
):
    rows, width = hidden.shape
    head_dim = w_keyval.shape[1] // 2
    inner = w_query.shape[1]
    cols = w_output.shape[1] // nt
    power = (np.arange(LANES) % (head_dim // 2)) * 2.0 / head_dim
    freq = jnp.asarray((10000.0 ** (-power)).astype(np.float32)[None, :])
    node = node_cache.reshape(-1, LANES)
    leaf = leaf_cache.reshape(-1, LANES)
    body_rows = inner // LANES * rows
    dma = pltpu.SemaphoreType.DMA
    shapes = (
        jax.ShapeDtypeStruct((rows, cols), BF16),
        jax.ShapeDtypeStruct((rows, LANES), BF16),
    )
    operands = (
        hidden,
        norm_gain[None, :],
        freq,
        leaf_branch,
        branch_root,
        root_owner,
        branch_owner,
        root_len,
        branch_len,
        leaf_len,
        w_query,
        w_keyval,
        w_output,
        node,
        leaf,
    )
    mixed, entry = pl.pallas_call(
        functools.partial(kernel, n, nt),
        out_shape=shapes,
        in_specs=[pl.BlockSpec(memory_space=pltpu.HBM)] * len(operands),
        out_specs=(pl.BlockSpec(memory_space=pltpu.VMEM),) * 2,
        scratch_shapes=[
            *[pltpu.VMEM(a.shape, a.dtype) for a in operands[:3]],
            *[pltpu.SMEM(a.shape, a.dtype) for a in operands[3:10]],
            pltpu.VMEM(w_query.shape, BF16),
            pltpu.VMEM(w_keyval.shape, BF16),
            pltpu.VMEM((nt, inner, cols), BF16),
            pltpu.VMEM(node.shape, BF16),
            pltpu.VMEM(leaf.shape, BF16),
            pltpu.VMEM((n, body_rows, LANES), BF16),
            pltpu.VMEM((n, body_rows + 2 * rows, LANES), BF16),
            pltpu.VMEM((n, body_rows + 2 * rows, LANES), BF16),
            pltpu.VMEM((nt, cols // LANES * rows, LANES), BF16),
            pltpu.VMEM((nt, cols // LANES * rows, LANES), BF16),
            dma((10 + 8 + 2 + nt,)),
            dma((n,)),
            dma((n,)),
            dma((n,)),
            dma((n,)),
            dma((nt,)),
            dma((nt,)),
        ],
        compiler_params=pltpu.CompilerParams(
            collective_id=0, has_side_effects=True, vmem_limit_bytes=63 * 1024 * 1024
        ),
    )(*operands)
    anywhere = pl.BlockSpec(memory_space=pl.ANY)
    mixed, entry = pl.pallas_call(
        deliver,
        out_shape=shapes,
        in_specs=[anywhere] * 2,
        out_specs=(anywhere,) * 2,
        scratch_shapes=[dma((2,))],
        compiler_params=pltpu.CompilerParams(vmem_limit_bytes=63 * 1024 * 1024),
    )(mixed, entry)
    return (mixed, entry[:, None, :])


def solution(mesh):
    in_specs = (
        P("request", None),
        P(),
        P(None, "tensor"),
        P(None, "tensor"),
        P("tensor", None),
        P("request", "tensor", None, None),
        P("request", "tensor", None, None),
        P(),
        P(),
        P(),
        P(),
        P(),
        P(),
        P("request"),
    )
    out_specs = (P("request", "tensor"), P("request", "tensor", None))
    run = functools.partial(local, mesh.shape["request"], mesh.shape["tensor"])
    return jax.shard_map(run, mesh=mesh, in_specs=in_specs, out_specs=out_specs, check_vma=False)
```
